256 devices in a mesh: dp: 4 (over x), seq: 16 (over z, core), head: 4 (over y).
Axes of the slice: x: 4, y: 4, z: 8, core: 2. Of those that a mesh axis runs over, the one named last changes fastest.
Arguments:
- queries: bfloat16 [4, 4096, 2048], P('dp', 'seq', 'head'), may hold values from -5.5 to 5.5
- keys: bfloat16 [4, 4096, 2048], P('dp', 'seq', 'head'), may hold values from -5.5 to 5.5
- values: bfloat16 [4, 4096, 2048], P('dp', 'seq', 'head'), may hold values from -5.5 to 5.5
- out_weight: bfloat16 [2048, 2048], P('head'), may hold values from -0.125 to 0.125
- out_grad: bfloat16 [4, 4096, 2048], P('dp', 'seq', 'head'), may hold values from -6 to 6
Outputs:
- mixed: bfloat16 [4, 4096, 2048], P('dp', 'seq', 'head')
- grad_queries: bfloat16 [4, 4096, 2048], P('dp', 'seq', 'head')
- grad_keys: bfloat16 [4, 4096, 2048], P('dp', 'seq', 'head')
- grad_values: bfloat16 [4, 4096, 2048], P('dp', 'seq', 'head')
- grad_out_weight: float32 [2048, 2048], P('head', 'seq')
The draws below stay inside these ranges and needn't reach their ends.
All inputs are finite; a program needn't handle non-finite values.
Results may differ from the reference program's by a relative error of at most 0.025.
Values may be sent and summed in bfloat16 or wider, within the bound.
No kernel may reach another device: no remote copies, remote signals or barrier semaphores. Data moves between devices by JAX's collectives and lax.ppermute only.
A program may use at most 128 MiB of HBM per device.

```python
import math
import jax
import jax.numpy as jnp
import numpy as np
from jax import lax

D = 2048
HEADS = 16
DH = 128
NR = 128
C = 64
LEN_DEV = 256
LEVELS = 4
BATCH = 4
SEQ_LEN = 4096
N_SEQ = 16


def region_field(key, scale_now):
    region_draw = jax.random.normal(key, (BATCH, SEQ_LEN // 16, 1, D), jnp.float32)
    widened = jnp.broadcast_to(region_draw, (BATCH, SEQ_LEN // 16, 16, D))
    return widened.reshape(BATCH, SEQ_LEN, D) * scale_now


def rough_field(key):
    noise_key, region_key = jax.random.split(key)
    noise = jax.random.normal(noise_key, (BATCH, SEQ_LEN, D), jnp.float32)
    return 0.8 * noise + region_field(region_key, 0.6)


def draw_queries(key, part):
    own_key = jax.random.fold_in(key, 11)
    field = rough_field(own_key)
    return jnp.clip(field, -5.5, 5.5).astype(jnp.bfloat16)


def draw_keys(key, part):
    own_key = jax.random.fold_in(key, 12)
    field = rough_field(own_key)
    return jnp.clip(field, -5.5, 5.5).astype(jnp.bfloat16)


def draw_values(key, part):
    own_key = jax.random.fold_in(key, 13)
    field = rough_field(own_key)
    return jnp.clip(field, -5.5, 5.5).astype(jnp.bfloat16)


def with_spikes(array, key, source, target, blocks, factor):
    owner, partner = [(jnp.arange(array.shape[axis_at]) // (array.shape[axis_at] // blocks)).reshape([-1 if axis == axis_at else 1 for axis in range(array.ndim)]) for axis_at in (source, target)]
    chosen = jax.random.permutation(key, blocks)[partner]
    strong = (owner == chosen) | (owner == (partner + blocks // 2) % blocks)
    return jnp.where(strong, factor * array, array)


def shard_levels(rng, dims, shards, low, largest):
    level = 1.0
    for axis_at, blocks in shards:
        draws = jax.random.uniform(jax.random.fold_in(jax.random.fold_in(rng, 6), axis_at), (blocks,), jnp.float32, low / len(shards), largest / len(shards))
        level = level * jnp.repeat(jnp.exp(draws), dims[axis_at] // blocks).reshape((-1,) + (1,) * (len(dims) - 1 - axis_at))
    return level


def scatter_about(key, shape, width, bound, cuts=(), held_as=jnp.bfloat16):
    array = width * jax.random.normal(key, shape, jnp.float32)
    if cuts:
        array = array * shard_levels(key, shape, cuts, -0.22, 0.18)
    return jnp.clip(array, -bound, bound).astype(held_as)


def gaussian_with(key, extent, deviation, most, pieces, heavy, kind=jnp.bfloat16):
    result = deviation * jax.random.normal(key, extent, jnp.float32)
    if pieces:
        result = result * shard_levels(key, extent, pieces, -0.22, 0.18)
    return jnp.clip(with_spikes(result, jax.random.fold_in(key, 3), *heavy), -most, most).astype(kind)


def setup_inputs(seed: int = 0) -> dict:
    seeds = jax.random.split(jax.random.key(seed), 6)
    return {
        "queries": draw_queries(jax.random.fold_in(seeds[5], 71), 0),
        "keys": draw_keys(jax.random.fold_in(seeds[5], 71), 0),
        "values": draw_values(jax.random.fold_in(seeds[5], 71), 0),
        "out_weight": scatter_about(seeds[3], (D, D), D ** -0.5, 0.125, ((0, 4),)),
        "out_grad": gaussian_with(seeds[4], (BATCH, SEQ_LEN, D), 1.0, 6.0, ((0, 4), (1, 16), (2, 4)), (1, 2, 16, 2.0)),
    }


def round_half(source):
    return lax.optimization_barrier(source.astype(jnp.bfloat16)).astype(jnp.float32)

def head_pass(inputs):
    query_rows, key_rows, value_rows, attn_grad = inputs
    score_scale = 1.0 / math.sqrt(DH)
    group_size = LEN_DEV // C
    block_count = SEQ_LEN // NR
    coarse_rows = (LEVELS + 2) * C
    paired = jnp.concatenate([key_rows, value_rows], axis=1).astype(jnp.float32)
    pooled = []
    for section_index in range(LEVELS + 1):
        pooled.append(paired.reshape(N_SEQ >> section_index, C, group_size << section_index, 2 * DH).mean(axis=2))
    segment_ids = np.arange(N_SEQ)
    coarse_parts = [pooled[0]]
    for section_index in range(LEVELS):
        coarse_parts.append(pooled[section_index][segment_ids >> section_index ^ 1])
    coarse_parts.append(jnp.broadcast_to(pooled[LEVELS], (N_SEQ, C, 2 * DH)))
    coarse = round_half(jnp.concatenate(coarse_parts, axis=1))
    coarse_keys = coarse[:, :, :DH]
    coarse_values = coarse[:, :, DH:]
    padded = jnp.pad(paired, ((NR, NR), (0, 0))).reshape(block_count + 2, NR, 2 * DH)
    window = jnp.concatenate([padded[:-2], padded[1:-1], padded[2:]], axis=1)
    fine_keys = window[:, :, :DH]
    fine_values = window[:, :, DH:]
    slot_index = np.arange(block_count)[:, None] * NR + np.arange(3 * NR)[None, :]
    visible = (slot_index >= NR) & (slot_index < NR + SEQ_LEN)
    query_wide = query_rows.astype(jnp.float32).reshape(block_count, NR, DH)
    query_seg = query_wide.reshape(N_SEQ, LEN_DEV, DH)
    fine_scores = jnp.einsum('nqd,nkd->nqk', query_wide, fine_keys) * score_scale
    fine_scores = jnp.where(visible[:, None, :], fine_scores, -jnp.inf)
    coarse_scores = jnp.einsum('sqd,scd->sqc', query_seg, coarse_keys).reshape(block_count, NR, coarse_rows) * score_scale
    highest = jnp.maximum(lax.optimization_barrier(jnp.max(fine_scores, axis=-1)), lax.optimization_barrier(jnp.max(coarse_scores, axis=-1)))
    fine_exp = jnp.exp(fine_scores - highest[..., None])
    coarse_exp = jnp.exp(coarse_scores - highest[..., None])
    totals = lax.optimization_barrier(jnp.sum(fine_exp, axis=-1)) + lax.optimization_barrier(jnp.sum(coarse_exp, axis=-1))
    fine_probs = fine_exp / totals[..., None]
    coarse_probs = coarse_exp / totals[..., None]
    fine_weights = round_half(fine_probs)
    coarse_weights = round_half(coarse_probs)
    coarse_weights_seg = coarse_weights.reshape(N_SEQ, LEN_DEV, coarse_rows)
    attended = jnp.einsum('nqk,nkd->nqd', fine_weights, fine_values).reshape(SEQ_LEN, DH)
    attended = attended + jnp.einsum('sqc,scd->sqd', coarse_weights_seg, coarse_values).reshape(SEQ_LEN, DH)
    attended_half = attended.astype(jnp.bfloat16)
    attended_wide = round_half(attended)
    grad_wide = attn_grad.astype(jnp.float32)
    grad_blocks = grad_wide.reshape(block_count, NR, DH)
    grad_seg = grad_wide.reshape(N_SEQ, LEN_DEV, DH)
    row_delta = lax.optimization_barrier(jnp.sum(grad_wide * attended_wide, axis=1)).reshape(block_count, NR)
    fine_pgrad = jnp.einsum('nqd,nkd->nqk', grad_blocks, fine_values)
    coarse_pgrad = jnp.einsum('sqd,scd->sqc', grad_seg, coarse_values).reshape(block_count, NR, coarse_rows)
    fine_sgrad = round_half(fine_probs * (fine_pgrad - row_delta[..., None]) * score_scale)
    coarse_sgrad = round_half(coarse_probs * (coarse_pgrad - row_delta[..., None]) * score_scale)
    coarse_sgrad_seg = coarse_sgrad.reshape(N_SEQ, LEN_DEV, coarse_rows)
    grad_query = jnp.einsum('nqk,nkd->nqd', fine_sgrad, fine_keys).reshape(SEQ_LEN, DH)
    grad_query = grad_query + jnp.einsum('sqc,scd->sqd', coarse_sgrad_seg, coarse_keys).reshape(SEQ_LEN, DH)
    fine_kgrad = jnp.einsum('nqk,nqd->nkd', fine_sgrad, query_wide)
    fine_vgrad = jnp.einsum('nqk,nqd->nkd', fine_weights, grad_blocks)
    fine_grad = jnp.concatenate([fine_kgrad, fine_vgrad], axis=2).reshape(block_count, 3, NR, 2 * DH)
    extended = jnp.zeros((block_count + 2, NR, 2 * DH), jnp.float32)
    extended = extended.at[:-2].add(fine_grad[:, 0]).at[1:-1].add(fine_grad[:, 1]).at[2:].add(fine_grad[:, 2])
    token_grad = extended[1:-1].reshape(SEQ_LEN, 2 * DH)
    coarse_kgrad = jnp.einsum('sqc,sqd->scd', coarse_sgrad_seg, query_seg)
    coarse_vgrad = jnp.einsum('sqc,sqd->scd', coarse_weights_seg, grad_seg)
    coarse_grad = jnp.concatenate([coarse_kgrad, coarse_vgrad], axis=2)
    pooled_grads = [jnp.zeros_like(entry) for entry in pooled]
    pooled_grads[0] = pooled_grads[0] + coarse_grad[:, :C]
    for section_index in range(LEVELS):
        level_terms = coarse_grad[:, (section_index + 1) * C:(section_index + 2) * C]
        pooled_grads[section_index] = pooled_grads[section_index].at[segment_ids >> section_index ^ 1].add(level_terms)
    pooled_grads[LEVELS] = pooled_grads[LEVELS] + lax.optimization_barrier(jnp.sum(coarse_grad[:, (LEVELS + 1) * C:], axis=0))[None]
    for section_index in range(LEVELS + 1):
        repeat_count = group_size << section_index
        widened = jnp.broadcast_to(pooled_grads[section_index][:, :, None, :], (N_SEQ >> section_index, C, repeat_count, 2 * DH))
        token_grad = token_grad + widened.reshape(SEQ_LEN, 2 * DH) / repeat_count
    return (attended_half, grad_query.astype(jnp.bfloat16), token_grad[:, :DH].astype(jnp.bfloat16), token_grad[:, DH:].astype(jnp.bfloat16))

def split_heads(source):
    return source.reshape(BATCH, SEQ_LEN, HEADS, DH).transpose(0, 2, 1, 3).reshape(BATCH * HEADS, SEQ_LEN, DH)

def merge_heads(source):
    return source.reshape(BATCH, HEADS, SEQ_LEN, DH).transpose(0, 2, 1, 3).reshape(BATCH, SEQ_LEN, HEADS * DH)

def reference(queries, keys, values, out_weight, out_grad):
    flat_grad = out_grad.reshape(BATCH * SEQ_LEN, D)
    attn_grad = jnp.dot(flat_grad, out_weight.T, preferred_element_type=jnp.float32).astype(jnp.bfloat16)
    attn_grad = attn_grad.reshape(BATCH, SEQ_LEN, D)
    results = lax.map(head_pass, (split_heads(queries), split_heads(keys), split_heads(values), split_heads(attn_grad)))
    attended, grad_queries, grad_keys, grad_values = [merge_heads(entry) for entry in results]
    flat_attended = attended.reshape(BATCH * SEQ_LEN, D)
    mixed = jnp.dot(flat_attended, out_weight, preferred_element_type=jnp.float32).astype(jnp.bfloat16)
    grad_out_weight = jnp.dot(flat_attended.T, flat_grad, preferred_element_type=jnp.float32)
    return (mixed.reshape(BATCH, SEQ_LEN, D), grad_queries, grad_keys, grad_values, grad_out_weight)
```

```python
import functools
import math

import jax
import jax.numpy as jnp
from jax import lax
from jax.experimental import pallas as pl
from jax.experimental.pallas import tpu as pltpu
from jax.sharding import Mesh, PartitionSpec as P

DH = 128
NR = 128
C = 64
HEADS = 4
ROWS = 256
WIDTH = 512
KEYS = 896
COARSE = 384
JOINT = 768
BF = jnp.bfloat16
F32 = jnp.float32
SCALE = 1.0 / math.sqrt(DH)
LOG2E = math.log2(math.e)
LIMIT = 40 * 1024 * 1024


def params(**kw):
    return pltpu.CompilerParams(vmem_limit_bytes=LIMIT, **kw)


def pool_matrix(rows, positions, flip=False):
    shape = (positions, rows) if flip else (rows, positions)
    r = lax.broadcasted_iota(jnp.int32, shape, 1 if flip else 0)
    p = lax.broadcasted_iota(jnp.int32, shape, 0 if flip else 1)
    l0 = (r < 64) & ((p >> 2) == r)
    l1 = (r >= 64) & (r < 96) & ((p >> 3) == r - 64)
    l2 = (r >= 96) & (r < 112) & ((p >> 4) == r - 96)
    l3 = (r >= 112) & (r < 120) & ((p >> 5) == r - 112)
    out = jnp.where(l0, 0.25, 0.0) + jnp.where(l1, 0.125, 0.0)
    out = out + jnp.where(l2, 0.0625, 0.0) + jnp.where(l3, 0.03125, 0.0)
    return out.astype(BF)


def top_matrix():
    r = lax.broadcasted_iota(jnp.int32, (64, 320), 0)
    j = lax.broadcasted_iota(jnp.int32, (64, 320), 1)
    l0 = (j < 128) & ((j >> 4) == r)
    l1 = (j >= 128) & (j < 192) & (8 + ((j - 128) >> 3) == r)
    l2 = (j >= 192) & (j < 256) & (16 + ((j - 192) >> 2) == r)
    l3 = (j >= 256) & (32 + ((j - 256) >> 1) == r)
    out = jnp.where(l0, 0.0625, 0.0) + jnp.where(l1, 0.125, 0.0)
    out = out + jnp.where(l2, 0.25, 0.0) + jnp.where(l3, 0.5, 0.0)
    return out.astype(BF)


def dot(a, b, dims):
    return lax.dot_general(a, b, (dims, ((), ())), preferred_element_type=F32)


NN = ((1,), (0,))
NT = ((1,), (1,))
TN = ((0,), (0,))


def prep_kernel(where_ref, k_ref, v_ref, own_ref, near_ref, far_ref, last_ref, first_ref):
    z = where_ref[0]
    m = pool_matrix(128, ROWS)
    for part, ref in enumerate((k_ref, v_ref)):
        x = ref[...]
        pooled = dot(m, x, NN).astype(BF)
        own_ref[part] = pooled[0:64]
        near_ref[part] = pooled[64:96]
        mid, low = pooled[96:112], pooled[112:128]
        for j in range(8):
            far_ref[j, part] = jnp.where((z ^ j) >= 4, low, mid)
        last_ref[part] = x[ROWS - NR :]
        first_ref[part] = x[:NR]


def fwd_kernel(
    where_ref, q_ref, k_ref, v_ref, prev_ref, next_ref, own_ref, sib_ref, near_ref, nearo_ref,
    far_ref, faro_ref, att_ref, attt_ref, prob_ref, keys_ref, vals_ref,
):
    z, s = where_ref[0], where_ref[2]
    top = top_matrix()
    for part, ref, out in ((0, k_ref, keys_ref), (1, v_ref, vals_ref)):
        out[0, 0:128] = prev_ref[part]
        out[0, 128:384] = ref[...]
        out[0, 384:448] = own_ref[part]
        out[0, 448:512] = sib_ref[part]
        out[0, 512:544] = near_ref[part]
        out[0, 544:576] = nearo_ref[part]
        for d in (2, 3):
            at = 576 + (d - 2) * 32
            out[0, at : at + 16] = far_ref[z ^ d, part]
            out[0, at + 16 : at + 32] = faro_ref[z ^ d, part]
        for d in range(4, 8):
            at = 640 + (d - 4) * 16
            both = jnp.concatenate([far_ref[z ^ d, part][0:8], faro_ref[z ^ d, part][0:8]], axis=0)
            out[0, at : at + 16] = both
        out[0, 704:768] = dot(top, out[0, 384:704], NN).astype(BF)
        out[0, 768:896] = next_ref[part]
    col = lax.broadcasted_iota(jnp.int32, (1, JOINT), 1)
    for n in range(2):
        q = q_ref[n * NR : (n + 1) * NR]
        scores = dot(q, keys_ref[0, n * NR : n * NR + JOINT], NT)
        if n == 0:
            hidden = (col < NR) & (s == 0)
        else:
            hidden = (col >= JOINT - NR) & (s == 15)
        scores = jnp.where(hidden, -jnp.inf, scores)
        highest = jnp.max(scores, axis=1, keepdims=True)
        e = jnp.exp2((scores - highest) * (SCALE * LOG2E))
        p = (e * (1.0 / jnp.sum(e, axis=1, keepdims=True))).astype(BF)
        prob_ref[0, n] = p
        att = dot(p, vals_ref[0, n * NR : n * NR + JOINT], NN)
        att_ref[n * NR : (n + 1) * NR] = att.astype(BF)
        attt_ref[:, n * NR : (n + 1) * NR] = att.T.astype(BF)


def wgrad_kernel(where_ref, attt_ref, og_ref, mine_ref, theirs_ref):
    c = where_ref[1]
    r = dot(attt_ref[...], og_ref[...], NN)
    lo, hi = r[:, :128].astype(BF), r[:, 128:].astype(BF)
    mine = jnp.where(c == 0, lo, hi)
    theirs = jnp.where(c == 0, hi, lo)
    for i in range(4):
        mine_ref[i, 0] = mine[i * 128 : (i + 1) * 128]
        theirs_ref[i, 0] = theirs[i * 128 : (i + 1) * 128]


def proj_kernel(att_ref, og_ref, w_ref, mix_ref, gatt_ref, acc_ref):
    j = pl.program_id(0)
    w = w_ref[...]
    mix_ref[...] = dot(att_ref[...], w, NN).astype(BF)
    term = dot(og_ref[...], w, NT)

    @pl.when(j == 0)
    def _():
        acc_ref[...] = term

    @pl.when(j > 0)
    def _():
        acc_ref[...] += term

    gatt_ref[...] = acc_ref[...].astype(BF)


def route_kernel(where_ref, mine_ref, got_ref, own_ref, up_ref, down_ref, across_ref):
    me = where_ref[3]
    for shift, out in ((0, own_ref), (1, up_ref), (3, down_ref), (2, across_ref)):
        i = (me + shift) & 3
        out[...] = (mine_ref[i].astype(F32) + got_ref[i].astype(F32)).astype(BF)


def bwd_kernel(
    q_ref, da_ref, att_ref, prob_ref, keys_ref, vals_ref,
    dq_ref, mid_ref, toprev_ref, tonext_ref, own_ref, cross_ref, minec_ref, gk_ref, gv_ref,
):
    gk_ref[768:896] = jnp.zeros((128, DH), F32)
    gv_ref[768:896] = jnp.zeros((128, DH), F32)
    for n in range(2):
        rows = slice(n * NR, (n + 1) * NR)
        span = slice(n * NR, n * NR + JOINT)
        q, da = q_ref[rows], da_ref[rows]
        delta = jnp.sum(da.astype(F32) * att_ref[rows].astype(F32), axis=1, keepdims=True)
        p = prob_ref[0, n]
        pgrad = dot(da, vals_ref[0, span], NT)
        sgrad = (p.astype(F32) * ((pgrad - delta) * SCALE)).astype(BF)
        dq_ref[rows] = dot(sgrad, keys_ref[0, span], NN).astype(BF)
        gk = dot(sgrad, q, TN)
        gv = dot(p, da, TN)
        if n == 0:
            gk_ref[0:768] = gk
            gv_ref[0:768] = gv
        else:
            gk_ref[span] += gk
            gv_ref[span] += gv
    top = top_matrix()
    for part, g in ((0, gk_ref), (1, gv_ref)):
        high = g[704:768]
        hi = high.astype(BF)
        lo = (high - hi.astype(F32)).astype(BF)
        g[384:704] += dot(top, hi, TN) + dot(top, lo, TN)
        toprev_ref[part] = g[0:128].astype(BF)
        mid_ref[part] = g[128:384]
        tonext_ref[part] = g[768:896].astype(BF)
        own_ref[part] = g[384:448]
        cross_ref[part, 0:64] = g[448:512].astype(BF)
        cross_ref[part, 64:96] = g[544:576].astype(BF)
        minec_ref[part, 0:32] = g[512:544]
        for d in (2, 3):
            at, to = 576 + (d - 2) * 32, 32 + (d - 2) * 16
            minec_ref[part, to : to + 16] = g[at : at + 16]
            cross_ref[part, 64 + to : 64 + to + 16] = g[at + 16 : at + 32].astype(BF)
        for d in (4, 6):
            at, to = 640 + (d - 4) * 16, 64 + (d - 4) * 8
            minec_ref[part, to : to + 8] = g[at : at + 8]
            minec_ref[part, to + 8 : to + 16] = g[at + 16 : at + 24]
            both = jnp.concatenate([g[at + 8 : at + 16], g[at + 24 : at + 32]], axis=0)
            cross_ref[part, 64 + to : 64 + to + 16] = both.astype(BF)


def gather_kernel(where_ref, minec_ref, got_ref, near_ref, far_ref):
    z = where_ref[0]
    for part in range(2):
        total = minec_ref[part] + got_ref[part, 64:160].astype(F32)
        near_ref[part] = total[0:32].astype(BF)
        far_ref[z, part] = jnp.zeros((16, WIDTH), BF)
        far_ref[z ^ 1, part] = jnp.zeros((16, WIDTH), BF)
        for d in (2, 3):
            at = 32 + (d - 2) * 16
            far_ref[z ^ d, part] = total[at : at + 16].astype(BF)
        for d in range(4, 8):
            at = 64 + (d - 4) * 8
            piece = jnp.concatenate([total[at : at + 8], jnp.zeros((8, WIDTH), F32)], axis=0)
            far_ref[z ^ d, part] = piece.astype(BF)


def sum_kernel(a_ref, b_ref, c_ref, d_ref, out_ref):
    total = a_ref[...].astype(F32) + b_ref[...].astype(F32)
    out_ref[...] = (total + c_ref[...].astype(F32) + d_ref[...].astype(F32)).astype(BF)


def sum8_kernel(a_ref, out_ref):
    total = a_ref[0].astype(F32)
    for j in range(1, 8):
        total = total + a_ref[j].astype(F32)
    out_ref[...] = total.astype(BF)


def final_kernel(
    where_ref, mid_ref, own_ref, got_ref, near_ref, far_ref, below_ref, above_ref, gk_ref, gv_ref
):
    z = where_ref[0]
    m = pool_matrix(128, ROWS, flip=True)
    for part, out in ((0, gk_ref), (1, gv_ref)):
        l0 = own_ref[part] + got_ref[part, 0:64].astype(F32)
        l1 = near_ref[part].astype(F32)
        l2 = far_ref[z ^ 2, part].astype(F32) + far_ref[z ^ 3, part].astype(F32)
        l3 = far_ref[z ^ 4, part].astype(F32) + far_ref[z ^ 5, part].astype(F32)
        l3 = l3 + far_ref[z ^ 6, part].astype(F32) + far_ref[z ^ 7, part].astype(F32)
        stack = jnp.concatenate([l0, l1, l2, l3], axis=0)
        hi = stack.astype(BF)
        lo = (stack - hi.astype(F32)).astype(BF)
        spread = dot(m, hi, NN) + dot(m, lo, NN)
        total = mid_ref[part] + spread
        out[0:128] = (total[0:128] + below_ref[part].astype(F32)).astype(BF)
        out[128:256] = (total[128:256] + above_ref[part].astype(F32)).astype(BF)


def sds(shape, dtype):
    return jax.ShapeDtypeStruct(shape, dtype)


def smem():
    return pl.BlockSpec(memory_space=pltpu.SMEM)


def vmem():
    return pl.BlockSpec(memory_space=pltpu.VMEM)


def cost(flops, size):
    return pl.CostEstimate(flops=flops, bytes_accessed=size, transcendentals=0)


def whole(kernel, scalars, arrays, outs, estimate):
    return pl.pallas_call(
        kernel,
        out_shape=outs,
        in_specs=[smem()] * len(scalars) + [vmem()] * len(arrays),
        out_specs=[vmem()] * len(outs),
        compiler_params=params(),
        cost_estimate=estimate,
    )(*scalars, *arrays)


def permute(x, axis, move):
    size = lax.axis_size(axis)
    return lax.ppermute(x, axis, [(i, move(i) % size) for i in range(size)])


def body(queries, keys, values, out_weight, out_grad):
    z, core, dp = lax.axis_index("z"), lax.axis_index("core"), lax.axis_index("dp")
    where = jnp.stack([z, core, z * 2 + core, dp]).astype(jnp.int32)
    q, k, v = (x.reshape(ROWS, WIDTH) for x in (queries, keys, values))
    n_seq = 16
    up = [(i, i + 1) for i in range(n_seq - 1)]
    down = [(i + 1, i) for i in range(n_seq - 1)]
    seq = ("z", "core")
    swap = functools.partial(permute, axis="core", move=lambda i: i ^ 1)
    hop = functools.partial(permute, axis="z", move=lambda i: i ^ 1)

    og = lax.all_gather(out_grad.reshape(ROWS, WIDTH), "head", axis=1, tiled=True)

    own, near, far, last, first = whole(
        prep_kernel, [where], [k, v],
        [sds((2, 64, WIDTH), BF), sds((2, 32, WIDTH), BF), sds((8, 2, 16, WIDTH), BF),
         sds((2, NR, WIDTH), BF), sds((2, NR, WIDTH), BF)],
        cost(10**8, 2 * 10**6),
    )
    sib = swap(own)
    near_got = hop(near)
    prev = lax.ppermute(last, seq, up)
    after = lax.ppermute(first, seq, down)
    far_got = lax.all_to_all(far, "z", 0, 0)
    far_other = swap(far_got)
    near_other = swap(near_got)

    by_head = lambda rows: pl.BlockSpec((rows, DH), lambda h: (0, h))
    pair = lambda rows: pl.BlockSpec((2, rows, DH), lambda h: (0, 0, h))
    far_spec = pl.BlockSpec((8, 2, 16, DH), lambda h: (0, 0, 0, h))
    lead = lambda *dims: pl.BlockSpec((1,) + dims, lambda h: (h,) + (0,) * len(dims))
    att, attt, prob, kbuf, vbuf = pl.pallas_call(
        fwd_kernel,
        grid=(HEADS,),
        out_shape=[
            sds((ROWS, WIDTH), BF), sds((WIDTH, ROWS), BF), sds((HEADS, 2, NR, JOINT), BF),
            sds((HEADS, KEYS, DH), BF), sds((HEADS, KEYS, DH), BF),
        ],
        in_specs=[
            smem(), by_head(ROWS), by_head(ROWS), by_head(ROWS), pair(NR), pair(NR),
            pair(64), pair(64), pair(32), pair(32), far_spec, far_spec,
        ],
        out_specs=[
            by_head(ROWS), pl.BlockSpec((DH, ROWS), lambda h: (h, 0)), lead(2, NR, JOINT),
            lead(KEYS, DH), lead(KEYS, DH),
        ],
        compiler_params=params(),
        cost_estimate=cost(6 * 10**9, 4 * 10**6),
    )(where, q, k, v, prev, after, own, sib, near_got, near_other, far_got, far_other)

    piece = pl.BlockSpec((4, 1, 128, 128), lambda j: (0, j, 0, 0))
    mine, theirs = pl.pallas_call(
        wgrad_kernel,
        grid=(8,),
        out_shape=[sds((4, 8, 128, 128), BF)] * 2,
        in_specs=[smem(), vmem(), pl.BlockSpec((ROWS, 256), lambda j: (0, j))],
        out_specs=[piece, piece],
        compiler_params=params(),
        cost_estimate=cost(10**9, 3 * 10**6),
    )(where, attt, og)
    got = swap(theirs)

    mix, gatt = pl.pallas_call(
        proj_kernel,
        grid=(4,),
        out_shape=[sds((ROWS, 2048), BF), sds((ROWS, WIDTH), BF)],
        in_specs=[
            vmem(),
            pl.BlockSpec((ROWS, 512), lambda j: (0, j)),
            pl.BlockSpec((WIDTH, 512), lambda j: (0, j)),
        ],
        out_specs=[
            pl.BlockSpec((ROWS, 512), lambda j: (0, j)),
            pl.BlockSpec((ROWS, WIDTH), lambda j: (0, 0)),
        ],
        scratch_shapes=[pltpu.VMEM((ROWS, WIDTH), F32)],
        compiler_params=params(),
        cost_estimate=cost(2 * 10**9, 4 * 10**6),
    )(att, og, out_weight)
    mixed = lax.psum_scatter(mix, "head", scatter_dimension=1, tiled=True)

    kept, to_up, to_down, to_across = whole(
        route_kernel, [where], [mine, got], [sds((8, 128, 128), BF)] * 4, cost(10**6, 3 * 10**6)
    )
    from_down = permute(to_up, "dp", lambda i: i + 1)
    from_up = permute(to_down, "dp", lambda i: i - 1)
    from_across = permute(to_across, "dp", lambda i: i + 2)

    dq, mid, toprev, tonext, own_grad, cross, minec = pl.pallas_call(
        bwd_kernel,
        grid=(HEADS,),
        out_shape=[
            sds((ROWS, WIDTH), BF), sds((2, ROWS, WIDTH), F32), sds((2, NR, WIDTH), BF),
            sds((2, NR, WIDTH), BF), sds((2, 64, WIDTH), F32), sds((2, 160, WIDTH), BF),
            sds((2, 96, WIDTH), F32),
        ],
        in_specs=[
            by_head(ROWS), by_head(ROWS), by_head(ROWS), lead(2, NR, JOINT), lead(KEYS, DH),
            lead(KEYS, DH),
        ],
        out_specs=[by_head(ROWS), pair(ROWS), pair(NR), pair(NR), pair(64), pair(160), pair(96)],
        scratch_shapes=[pltpu.VMEM((KEYS, DH), F32)] * 2,
        compiler_params=params(),
        cost_estimate=cost(6 * 10**9, 5 * 10**6),
    )(q, gatt, att, prob, kbuf, vbuf)
    cross_got = swap(cross)
    above = lax.ppermute(toprev, seq, down)
    below = lax.ppermute(tonext, seq, up)
    near_grad, far_grad = whole(
        gather_kernel, [where], [minec, cross_got],
        [sds((2, 32, WIDTH), BF), sds((8, 2, 16, WIDTH), BF)], cost(10**6, 10**6),
    )
    near_back = hop(near_grad)

    (wsum,) = whole(
        sum_kernel, [], [kept, from_down, from_up, from_across], [sds((8, 128, 128), BF)],
        cost(10**6, 10**6),
    )
    wsum_got = lax.all_to_all(wsum, "z", 0, 0)
    far_back = lax.all_to_all(far_grad, "z", 0, 0)
    (wpart,) = whole(sum8_kernel, [], [wsum_got], [sds((128, 128), BF)], cost(10**6, 10**5))
    wall = lax.all_gather(wpart, "dp", axis=0, tiled=True)
    grad_out_weight = wall.astype(F32)

    grad_keys, grad_values = whole(
        final_kernel, [where],
        [mid, own_grad, cross_got, near_back, far_back, below, above],
        [sds((ROWS, WIDTH), BF)] * 2, cost(10**8, 3 * 10**6),
    )
    shape = (1, ROWS, WIDTH)
    return (
        mixed.reshape(shape), dq.reshape(shape), grad_keys.reshape(shape),
        grad_values.reshape(shape), grad_out_weight,
    )


def solution(mesh):
    dp, seq, head = (mesh.shape[name] for name in ("dp", "seq", "head"))
    cut = Mesh(mesh.devices.reshape(dp, seq // 2, 2, head), ("dp", "z", "core", "head"))
    rows = P("dp", ("z", "core"), "head")
    return jax.shard_map(
        body,
        mesh=cut,
        in_specs=(rows, rows, rows, P("head", None), rows),
        out_specs=(rows, rows, rows, rows, P("head", ("z", "core"))),
        check_vma=False,
    )
```

```python
import functools
import math

import jax
import jax.numpy as jnp
from jax import lax
from jax.experimental import pallas as pl
from jax.experimental.pallas import tpu as pltpu
from jax.sharding import Mesh, PartitionSpec as P

DH = 128
NR = 128
C = 64
HEADS = 4
ROWS = 256
WIDTH = 512
NEAR = 704
JOINT = 576
FAR = 192
BF = jnp.bfloat16
F32 = jnp.float32
LIMIT = 36 * 1024 * 1024
SCALE = 1.0 / math.sqrt(DH)
LOG2E = math.log2(math.e)


def pool_matrix(rows, positions, flip=False):
    shape = (positions, rows) if flip else (rows, positions)
    r = lax.broadcasted_iota(jnp.int32, shape, 1 if flip else 0)
    p = lax.broadcasted_iota(jnp.int32, shape, 0 if flip else 1)
    l0 = (r < 64) & ((p >> 2) == r)
    l1 = (r >= 64) & (r < 96) & ((p >> 3) == r - 64)
    l2 = (r >= 96) & (r < 112) & ((p >> 4) == r - 96)
    l3 = (r >= 112) & (r < 120) & ((p >> 5) == r - 112)
    out = jnp.where(l0, 0.25, 0.0) + jnp.where(l1, 0.125, 0.0)
    out = out + jnp.where(l2, 0.0625, 0.0) + jnp.where(l3, 0.03125, 0.0)
    return out.astype(BF)


def top_near():
    r = lax.broadcasted_iota(jnp.int32, (64, 192), 0)
    j = lax.broadcasted_iota(jnp.int32, (64, 192), 1)
    l0 = (j < 128) & ((j >> 4) == r)
    l1 = (j >= 128) & (8 + ((j - 128) >> 3) == r)
    return (jnp.where(l0, 0.0625, 0.0) + jnp.where(l1, 0.125, 0.0)).astype(BF)


def top_far():
    r = lax.broadcasted_iota(jnp.int32, (64, 128), 0)
    j = lax.broadcasted_iota(jnp.int32, (64, 128), 1)
    l2 = (j < 64) & (16 + (j >> 2) == r)
    l3 = (j >= 64) & (32 + ((j - 64) >> 1) == r)
    return (jnp.where(l2, 0.25, 0.0) + jnp.where(l3, 0.5, 0.0)).astype(BF)


def dot(a, b, dims):
    return lax.dot_general(a, b, (dims, ((), ())), preferred_element_type=F32)


NN = ((1,), (0,))
NT = ((1,), (1,))
TN = ((0,), (0,))


def prep_kernel(
    q_hbm, k_hbm, v_hbm, qkv_ref, own_ref, near_ref, far_ref, last_ref, first_ref, sems
):
    z = lax.axis_index("z")
    copies = [
        pltpu.make_async_copy(src, qkv_ref.at[at], sems.at[at])
        for at, src in ((1, k_hbm), (2, v_hbm), (0, q_hbm))
    ]
    for copy in copies:
        copy.start()
    m = pool_matrix(128, ROWS)
    for part in range(2):
        copies[part].wait()
        x = qkv_ref[1 + part]
        pooled = dot(m, x, NN).astype(BF)
        own_ref[part] = pooled[0:64]
        near_ref[part] = pooled[64:96]
        for d in range(8):
            far_ref[z ^ d, part] = pooled[112:128] if d >= 4 else pooled[96:112]
        last_ref[part] = x[ROWS - NR :]
        first_ref[part] = x[:NR]
    copies[2].wait()


def near_kernel(
    qkv_ref, prev_ref, next_ref, own_ref, sib_ref, near_ref, nearo_ref,
    keys_ref, vals_ref, exps_ref, part_ref, max_ref, sum_ref,
):
    s = lax.axis_index("z") * 2 + lax.axis_index("core")
    col = lax.broadcasted_iota(jnp.int32, (1, JOINT), 1)
    for h in range(HEADS):
        at_h = slice(h * DH, (h + 1) * DH)
        for part, out in ((0, keys_ref), (1, vals_ref)):
            out[h, 0:128] = prev_ref[part, :, at_h]
            out[h, 128:384] = qkv_ref[1 + part, :, at_h]
            out[h, 384:448] = own_ref[part, :, at_h]
            out[h, 448:512] = sib_ref[part, :, at_h]
            out[h, 512:544] = near_ref[part, :, at_h]
            out[h, 544:576] = nearo_ref[part, :, at_h]
            out[h, 576:704] = next_ref[part, :, at_h]
        for n in range(2):
            rows = slice(n * NR, (n + 1) * NR)
            span = slice(n * NR, n * NR + JOINT)
            scores = dot(qkv_ref[0, rows, at_h], keys_ref[h, span], NT)
            if n == 0:
                hidden = (col < NR) & (s == 0)
            else:
                hidden = (col >= JOINT - NR) & (s == 15)
            scores = jnp.where(hidden, -jnp.inf, scores)
            highest = jnp.max(scores, axis=1, keepdims=True)
            e = jnp.exp2((scores - highest) * (SCALE * LOG2E))
            max_ref[h, rows] = highest
            sum_ref[h, rows] = jnp.sum(e, axis=1, keepdims=True)
            e = e.astype(BF)
            exps_ref[h, n] = e
            part_ref[rows, at_h] = dot(e, vals_ref[h, span], NN)


def far_kernel(
    qkv_ref, far_ref, faro_ref, keys_ref, vals_ref, part_ref, max_ref, sum_ref,
    att_ref, attt_ref, exps_ref, fkeys_ref, fvals_ref, rnear_ref, rfar_ref,
):
    z = lax.axis_index("z")
    by_near, by_far = top_near(), top_far()
    for h in range(HEADS):
        at_h = slice(h * DH, (h + 1) * DH)
        for part, near, out in ((0, keys_ref, fkeys_ref), (1, vals_ref, fvals_ref)):
            for d in (2, 3):
                at = (d - 2) * 32
                out[h, at : at + 16] = far_ref[z ^ d, part, :, at_h]
                out[h, at + 16 : at + 32] = faro_ref[z ^ d, part, :, at_h]
            for d in range(4, 8):
                at = 64 + (d - 4) * 16
                low, high = far_ref[z ^ d, part, :, at_h], faro_ref[z ^ d, part, :, at_h]
                out[h, at : at + 16] = jnp.concatenate([low[0:8], high[0:8]], axis=0)
            top = dot(by_near, near[h, 384:576], NN) + dot(by_far, out[h, 0:128], NN)
            out[h, 128:192] = top.astype(BF)
        scores = dot(qkv_ref[0, :, at_h], fkeys_ref[h], NT)
        first = max_ref[h]
        highest = jnp.maximum(first, jnp.max(scores, axis=1, keepdims=True))
        e = jnp.exp2((scores - highest) * (SCALE * LOG2E))
        kept = jnp.exp2((first - highest) * (SCALE * LOG2E))
        inverse = 1.0 / (kept * sum_ref[h] + jnp.sum(e, axis=1, keepdims=True))
        e = e.astype(BF)
        exps_ref[h] = e
        rnear_ref[h] = kept * inverse
        rfar_ref[h] = inverse
        att = part_ref[:, at_h] * (kept * inverse) + dot(e, fvals_ref[h], NN) * inverse
        att_ref[:, at_h] = att.astype(BF)
        attt_ref[at_h, :] = att.T.astype(BF)


def wgrad_kernel(attt_ref, og0_ref, og1_ref, og2_ref, og3_ref, mine_ref, theirs_ref):
    c, me = lax.axis_index("core"), lax.axis_index("head")
    for shift, og_ref in enumerate((og0_ref, og1_ref, og2_ref, og3_ref)):
        j = (me + shift) & 3
        r = dot(attt_ref[...], og_ref[...], NN).astype(BF)
        for i in range(4):
            for t in range(2):
                lo = r[i * 128 : (i + 1) * 128, t * 256 : t * 256 + 128]
                hi = r[i * 128 : (i + 1) * 128, t * 256 + 128 : t * 256 + 256]
                mine_ref[i, 2 * j + t] = jnp.where(c == 0, lo, hi)
                theirs_ref[i, 2 * j + t] = jnp.where(c == 0, hi, lo)


def proj_kernel(
    _, att_ref, w_hbm, og0_ref, og1_ref, og2_ref, og3_ref,
    mix0_ref, mix1_ref, mix2_ref, mix3_ref, gatt_ref, w_ref, sems,
):
    me = lax.axis_index("head")
    copies = []
    for shift in range(4):
        at = pl.multiple_of(((me + shift) & 3) * 512, 512)
        copies.append(
            pltpu.make_async_copy(w_hbm.at[:, pl.ds(at, 512)], w_ref.at[shift], sems.at[shift])
        )
    for copy in copies:
        copy.start()
    total = None
    outs = (mix0_ref, mix1_ref, mix2_ref, mix3_ref)
    for shift, og_ref in enumerate((og0_ref, og1_ref, og2_ref, og3_ref)):
        copies[shift].wait()
        w = w_ref[shift]
        outs[shift][...] = dot(att_ref[...], w, NN).astype(BF)
        term = dot(og_ref[...], w, NT)
        total = term if shift == 0 else total + term
    gatt_ref[...] = total.astype(BF)


def route_kernel(mine_ref, got_ref, own_ref, up_ref, down_ref, across_ref):
    me = lax.axis_index("dp")
    for shift, out in ((0, own_ref), (1, up_ref), (3, down_ref), (2, across_ref)):
        i = (me + shift) & 3
        out[...] = (mine_ref[i].astype(F32) + got_ref[i].astype(F32)).astype(BF)


def bwd_kernel(
    _, qkv_ref, da_ref, att_ref, exps_ref, fexps_ref, keys_ref, vals_ref, fkeys_ref, fvals_ref,
    rnear_ref, rfar_ref,
    dq_ref, mid_ref, toprev_ref, tonext_ref, own_ref, cross_ref, minec_ref, gk_ref, gv_ref,
):
    by_near, by_far = top_near(), top_far()
    for h in range(HEADS):
        at_h = slice(h * DH, (h + 1) * DH)
        q, da = qkv_ref[0, :, at_h], da_ref[:, at_h]
        att = att_ref[:, at_h].astype(F32)
        delta = jnp.sum(da.astype(F32) * att, axis=1, keepdims=True)
        p = fexps_ref[h].astype(F32) * rfar_ref[h]
        pgrad = dot(da, fvals_ref[h], NT)
        sgrad = (p * ((pgrad - delta) * SCALE)).astype(BF)
        dq = dot(sgrad, fkeys_ref[h], NN)
        fgk, fgv = dot(sgrad, q, TN), dot(p.astype(BF), da, TN)
        gk, gv = gk_ref.at[h], gv_ref.at[h]
        gk[576:704] = jnp.zeros((128, DH), F32)
        gv[576:704] = jnp.zeros((128, DH), F32)
        for n in range(2):
            rows = slice(n * NR, (n + 1) * NR)
            span = slice(n * NR, n * NR + JOINT)
            p = exps_ref[h, n].astype(F32) * rnear_ref[h, rows]
            pgrad = dot(da[rows], vals_ref[h, span], NT)
            sgrad = (p * ((pgrad - delta[rows]) * SCALE)).astype(BF)
            p = p.astype(BF)
            dq_ref[rows, at_h] = (dq[rows] + dot(sgrad, keys_ref[h, span], NN)).astype(BF)
            if n == 0:
                gk[0:576] = dot(sgrad, q[rows], TN)
                gv[0:576] = dot(p, da[rows], TN)
            else:
                gk[128:704] += dot(sgrad, q[rows], TN)
                gv[128:704] += dot(p, da[rows], TN)
        for part, g, f in ((0, gk, fgk), (1, gv, fgv)):
            high = f[128:192]
            hi = high.astype(BF)
            lo = (high - hi.astype(F32)).astype(BF)
            near = g[384:576] + dot(by_near, hi, TN) + dot(by_near, lo, TN)
            far = f[0:128] + dot(by_far, hi, TN) + dot(by_far, lo, TN)
            toprev_ref[part, :, at_h] = g[0:128].astype(BF)
            mid_ref[part, :, at_h] = g[128:384]
            tonext_ref[part, :, at_h] = g[576:704].astype(BF)
            own_ref[part, :, at_h] = near[0:64]
            cross_ref[part, 0:64, at_h] = near[64:128].astype(BF)
            cross_ref[part, 64:96, at_h] = near[160:192].astype(BF)
            minec_ref[part, 0:32, at_h] = near[128:160]
            for d in (2, 3):
                at, to = (d - 2) * 32, 32 + (d - 2) * 16
                minec_ref[part, to : to + 16, at_h] = far[at : at + 16]
                cross_ref[part, 64 + to : 64 + to + 16, at_h] = far[at + 16 : at + 32].astype(BF)
            for d in (4, 6):
                at, to = 64 + (d - 4) * 16, 64 + (d - 4) * 8
                minec_ref[part, to : to + 8, at_h] = far[at : at + 8]
                minec_ref[part, to + 8 : to + 16, at_h] = far[at + 16 : at + 24]
                both = jnp.concatenate([far[at + 8 : at + 16], far[at + 24 : at + 32]], axis=0)
                cross_ref[part, 64 + to : 64 + to + 16, at_h] = both.astype(BF)


def merge_kernel(_, __, wsum_ref, minec_ref, got_ref, near_ref, out_ref):
    z = lax.axis_index("z")
    out_ref[:, 0:128] = wsum_ref[...]
    none = jnp.zeros((128, 128), BF)
    out_ref[z, 128:256] = none
    out_ref[z ^ 1, 128:256] = none
    for part in range(2):
        total = (minec_ref[part] + got_ref[part, 64:160].astype(F32)).astype(BF)
        near_ref[part] = total[0:32]
        low = total[64:96]
        for d in range(2, 8):
            if d < 4:
                piece = total[32 + (d - 2) * 16 : 48 + (d - 2) * 16]
            else:
                piece = low[(d - 4) * 8 : (d - 4) * 8 + 8]
                piece = jnp.concatenate([piece, jnp.zeros((8, WIDTH), BF)], axis=0)
            for col in range(4):
                at = 128 + part * 64 + col * 16
                out_ref[z ^ d, at : at + 16] = piece[:, col * 128 : (col + 1) * 128]


def sum_kernel(a_ref, b_ref, c_ref, d_ref, out_ref):
    total = a_ref[...].astype(F32) + b_ref[...].astype(F32)
    total = total + c_ref[...].astype(F32) + d_ref[...].astype(F32)
    out_ref[...] = total.astype(BF)


def sum8_kernel(a_ref, _, out_ref):
    total = a_ref[0, 0:128].astype(F32)
    for j in range(1, 8):
        total = total + a_ref[j, 0:128].astype(F32)
    for i in range(4):
        out_ref[i] = total.astype(BF)


def final_kernel(
    mid_ref, own_ref, got_ref, near_ref, far_ref, below_ref, above_ref, _,
    gk_ref, gv_ref,
):
    z = lax.axis_index("z")
    m = pool_matrix(128, ROWS, flip=True)
    for part, out in ((0, gk_ref), (1, gv_ref)):
        l0 = own_ref[part] + got_ref[part, 0:64].astype(F32)
        l1 = near_ref[part].astype(F32)
        base = 128 + part * 64
        far = [far_ref[z ^ d, base : base + 64].astype(F32) for d in range(2, 8)]
        l2, l3 = far[0] + far[1], far[2] + far[3] + far[4] + far[5]
        l2 = jnp.concatenate([l2[i * 16 : (i + 1) * 16] for i in range(4)], axis=1)
        l3 = jnp.concatenate([l3[i * 16 : (i + 1) * 16] for i in range(4)], axis=1)
        stack = jnp.concatenate([l0, l1, l2, l3], axis=0)
        hi = stack.astype(BF)
        lo = (stack - hi.astype(F32)).astype(BF)
        spread = dot(m, hi, NN) + dot(m, lo, NN)
        total = mid_ref[part] + spread
        out[0:128] = (total[0:128] + below_ref[part].astype(F32)).astype(BF)
        out[128:256] = (total[128:256] + above_ref[part].astype(F32)).astype(BF)


def sds(shape, dtype):
    return jax.ShapeDtypeStruct(shape, dtype)


HBM = pl.BlockSpec(memory_space=pltpu.HBM)
VMEM = pl.BlockSpec(memory_space=pltpu.VMEM)
AFTER = pl.BlockSpec(memory_space=pl.ANY)


def call(kernel, operands, outs, scratch=(), us=1, limit=LIMIT):
    return pl.pallas_call(
        kernel,
        out_shape=outs,
        in_specs=[spec for spec, _ in operands],
        out_specs=[VMEM] * len(outs),
        scratch_shapes=list(scratch),
        compiler_params=pltpu.CompilerParams(vmem_limit_bytes=limit),
        cost_estimate=pl.CostEstimate(flops=us * 10**9, bytes_accessed=1, transcendentals=0),
    )(*[array for _, array in operands])


def here(*arrays):
    return [(VMEM, array) for array in arrays]


def permute(x, axis, move):
    size = lax.axis_size(axis)
    return lax.ppermute(x, axis, [(i, move(i) % size) for i in range(size)])


def body(queries, keys, values, out_weight, out_grad):
    q, k, v = (x.reshape(ROWS, WIDTH) for x in (queries, keys, values))
    n_seq = 16
    up = [(i, i + 1) for i in range(n_seq - 1)]
    down = [(i + 1, i) for i in range(n_seq - 1)]
    seq = ("z", "core")
    swap = functools.partial(permute, axis="core", move=lambda i: i ^ 1)
    hop = functools.partial(permute, axis="z", move=lambda i: i ^ 1)
    dma = pltpu.SemaphoreType.DMA

    og = out_grad.reshape(ROWS, WIDTH)

    qkv, own, near, far, last, first = call(
        prep_kernel, [(HBM, q), (HBM, k), (HBM, v)],
        [sds((3, ROWS, WIDTH), BF), sds((2, 64, WIDTH), BF), sds((2, 32, WIDTH), BF),
         sds((8, 2, 16, WIDTH), BF), sds((2, NR, WIDTH), BF), sds((2, NR, WIDTH), BF)],
        [dma((3,))], limit=62 * 1024 * 1024,
    )
    sib = swap(own)
    near_got = hop(near)
    near_other = swap(near_got)
    prev = lax.ppermute(last, seq, up)
    after = lax.ppermute(first, seq, down)
    far_got = lax.all_to_all(far, "z", 0, 0)
    far_other = swap(far_got)
    ogs = [og] + [permute(og, "head", lambda i, m=m: i - m) for m in (1, 2, 3)]

    column = sds((HEADS, ROWS, 1), F32)
    keys_near, vals_near, exps, part, top, total = call(
        near_kernel, here(qkv, prev, after, own, sib, near_got, near_other),
        [sds((HEADS, NEAR, DH), BF), sds((HEADS, NEAR, DH), BF), sds((HEADS, 2, NR, JOINT), BF),
         sds((ROWS, WIDTH), F32), column, column],
        us=20,
    )
    att, attt, far_exps, keys_far, vals_far, rnear, rfar = call(
        far_kernel, here(qkv, far_got, far_other, keys_near, vals_near, part, top, total),
        [sds((ROWS, WIDTH), BF), sds((WIDTH, ROWS), BF), sds((HEADS, ROWS, FAR), BF),
         sds((HEADS, FAR, DH), BF), sds((HEADS, FAR, DH), BF), column, column],
    )
    mine, theirs = call(wgrad_kernel, here(attt, *ogs), [sds((4, 8, 128, 128), BF)] * 2)
    got = swap(theirs)
    *mixes, gatt = call(
        proj_kernel, [(AFTER, mine), (VMEM, att), (HBM, out_weight)] + here(*ogs),
        [sds((ROWS, WIDTH), BF)] * 5, [pltpu.VMEM((4, WIDTH, 512), BF), dma((4,))],
    )
    mix_parts = [mixes[0]]
    mix_parts += [permute(mixes[m], "head", lambda i, m=m: i + m) for m in (1, 2, 3)]

    kept, to_up, to_down, to_across = call(
        route_kernel, here(mine, got), [sds((8, 128, 128), BF)] * 4
    )
    from_down = permute(to_up, "dp", lambda i: i + 1)
    from_up = permute(to_down, "dp", lambda i: i - 1)
    from_across = permute(to_across, "dp", lambda i: i + 2)

    dq, mid, toprev, tonext, own_grad, cross, minec = call(
        bwd_kernel,
        [(AFTER, kept)]
        + here(qkv, gatt, att, exps, far_exps, keys_near, vals_near, keys_far, vals_far)
        + here(rnear, rfar),
        [sds((ROWS, WIDTH), BF), sds((2, ROWS, WIDTH), F32), sds((2, NR, WIDTH), BF),
         sds((2, NR, WIDTH), BF), sds((2, 64, WIDTH), F32), sds((2, 160, WIDTH), BF),
         sds((2, 96, WIDTH), F32)],
        [pltpu.VMEM((HEADS, NEAR, DH), F32)] * 2, us=20,
    )
    cross_got = swap(cross)
    above = lax.ppermute(toprev, seq, down)
    below = lax.ppermute(tonext, seq, up)
    (wsum,) = call(
        sum_kernel, here(kept, from_down, from_up, from_across), [sds((8, 128, 128), BF)], us=8
    )
    near_grad, both = call(
        merge_kernel, [(AFTER, above), (AFTER, below)] + here(wsum, minec, cross_got),
        [sds((2, 32, WIDTH), BF), sds((8, 256, 128), BF)],
    )
    near_back = hop(near_grad)
    both_got = lax.all_to_all(both, "z", 0, 0)
    (mixed,) = call(sum_kernel, here(*mix_parts), [sds((ROWS, WIDTH), BF)])
    (wpart,) = call(
        sum8_kernel, here(both_got) + [(AFTER, mixed)], [sds((4, 128, 128), BF)]
    )
    wall = lax.all_to_all(wpart, "dp", 0, 0)
    grad_out_weight = wall.reshape(WIDTH, 128).astype(F32)

    grad_keys, grad_values = call(
        final_kernel,
        here(mid, own_grad, cross_got, near_back, both_got, below, above) + [(AFTER, wpart)],
        [sds((ROWS, WIDTH), BF)] * 2,
    )
    shape = (1, ROWS, WIDTH)
    return (
        mixed.reshape(shape), dq.reshape(shape), grad_keys.reshape(shape),
        grad_values.reshape(shape), grad_out_weight,
    )


def solution(mesh):
    dp, seq, head = (mesh.shape[name] for name in ("dp", "seq", "head"))
    cut = Mesh(mesh.devices.reshape(dp, seq // 2, 2, head), ("dp", "z", "core", "head"))
    rows = P("dp", ("z", "core"), "head")
    return jax.shard_map(
        body,
        mesh=cut,
        in_specs=(rows, rows, rows, P("head", None), rows),
        out_specs=(rows, rows, rows, rows, P("head", ("z", "core"))),
        check_vma=False,
    )
```

```python
import functools
import math

import jax
import jax.numpy as jnp
from jax import lax
from jax.experimental import pallas as pl
from jax.experimental.pallas import tpu as pltpu
from jax.sharding import Mesh, PartitionSpec as P

DH = 128
NR = 128
C = 64
HEADS = 4
ROWS = 256
WIDTH = 512
NEAR = 704
JOINT = 576
FAR = 192
BF = jnp.bfloat16
F32 = jnp.float32
LIMIT = 36 * 1024 * 1024
SCALE = 1.0 / math.sqrt(DH)
LOG2E = math.log2(math.e)


def pool_matrix(rows, positions, flip=False):
    shape = (positions, rows) if flip else (rows, positions)
    r = lax.broadcasted_iota(jnp.int32, shape, 1 if flip else 0)
    p = lax.broadcasted_iota(jnp.int32, shape, 0 if flip else 1)
    l0 = (r < 64) & ((p >> 2) == r)
    l1 = (r >= 64) & (r < 96) & ((p >> 3) == r - 64)
    l2 = (r >= 96) & (r < 112) & ((p >> 4) == r - 96)
    l3 = (r >= 112) & (r < 120) & ((p >> 5) == r - 112)
    out = jnp.where(l0, 0.25, 0.0) + jnp.where(l1, 0.125, 0.0)
    out = out + jnp.where(l2, 0.0625, 0.0) + jnp.where(l3, 0.03125, 0.0)
    return out.astype(BF)


def top_near():
    r = lax.broadcasted_iota(jnp.int32, (64, 192), 0)
    j = lax.broadcasted_iota(jnp.int32, (64, 192), 1)
    l0 = (j < 128) & ((j >> 4) == r)
    l1 = (j >= 128) & (8 + ((j - 128) >> 3) == r)
    return (jnp.where(l0, 0.0625, 0.0) + jnp.where(l1, 0.125, 0.0)).astype(BF)


def top_far():
    r = lax.broadcasted_iota(jnp.int32, (64, 128), 0)
    j = lax.broadcasted_iota(jnp.int32, (64, 128), 1)
    l2 = (j < 64) & (16 + (j >> 2) == r)
    l3 = (j >= 64) & (32 + ((j - 64) >> 1) == r)
    return (jnp.where(l2, 0.25, 0.0) + jnp.where(l3, 0.5, 0.0)).astype(BF)


def dot(a, b, dims):
    return lax.dot_general(a, b, (dims, ((), ())), preferred_element_type=F32)


NN = ((1,), (0,))
NT = ((1,), (1,))
TN = ((0,), (0,))


def prep_kernel(
    q_hbm, k_hbm, v_hbm, qkv_ref, chip_ref, near_ref, far_ref, edge_ref, sems
):
    z, c = lax.axis_index("z"), lax.axis_index("core")
    copies = [
        pltpu.make_async_copy(src, qkv_ref.at[at], sems.at[at])
        for at, src in ((1, k_hbm), (2, v_hbm), (0, q_hbm))
    ]
    for copy in copies:
        copy.start()
    m = pool_matrix(128, ROWS)
    for part in range(2):
        copies[part].wait()
        x = qkv_ref[1 + part]
        pooled = dot(m, x, NN).astype(BF)
        chip_ref[part, 0:64] = pooled[0:64]
        near_ref[part] = pooled[64:96]
        for d in range(8):
            far_ref[z ^ d, part] = pooled[112:128] if d >= 4 else pooled[96:112]
        chip_ref[part, 64:192] = jnp.where(c == 0, x[NR:], x[:NR])
        edge_ref[part] = jnp.where(c == 0, x[:NR], x[NR:])
    copies[2].wait()


def token_kernel(_, __, ___, out_ref):
    out_ref[...] = jnp.zeros_like(out_ref)


def near_kernel(
    _, qkv_ref, edge_ref, chip_ref, sib_ref, near_ref, nearo_ref,
    keys_ref, vals_ref, exps_ref, part_ref, max_ref, sum_ref,
):
    z, c = lax.axis_index("z"), lax.axis_index("core")
    s = z * 2 + c
    col = lax.broadcasted_iota(jnp.int32, (1, JOINT), 1)
    for h in range(HEADS):
        at_h = slice(h * DH, (h + 1) * DH)
        for part, out in ((0, keys_ref), (1, vals_ref)):
            beside, across = sib_ref[part, 64:192, at_h], edge_ref[part, :, at_h]
            out[h, 0:128] = jnp.where(c == 0, across, beside)
            out[h, 128:384] = qkv_ref[1 + part, :, at_h]
            out[h, 384:448] = chip_ref[part, 0:64, at_h]
            out[h, 448:512] = sib_ref[part, 0:64, at_h]
            out[h, 512:544] = near_ref[part, :, at_h]
            out[h, 544:576] = nearo_ref[part, :, at_h]
            out[h, 576:704] = jnp.where(c == 0, beside, across)
        for n in range(2):
            rows = slice(n * NR, (n + 1) * NR)
            span = slice(n * NR, n * NR + JOINT)
            scores = dot(qkv_ref[0, rows, at_h], keys_ref[h, span], NT)
            if n == 0:
                hidden = (col < NR) & (s == 0)
            else:
                hidden = (col >= JOINT - NR) & (s == 15)
            scores = jnp.where(hidden, -jnp.inf, scores)
            highest = jnp.max(scores, axis=1, keepdims=True)
            e = jnp.exp2((scores - highest) * (SCALE * LOG2E))
            max_ref[h, rows] = highest
            sum_ref[h, rows] = jnp.sum(e, axis=1, keepdims=True)
            e = e.astype(BF)
            exps_ref[h, n] = e
            part_ref[rows, at_h] = dot(e, vals_ref[h, span], NN)


def far_kernel(
    qkv_ref, far_ref, faro_ref, keys_ref, vals_ref, part_ref, max_ref, sum_ref,
    att_ref, attt_ref, exps_ref, fkeys_ref, fvals_ref, rnear_ref, rfar_ref,
):
    z = lax.axis_index("z")
    by_near, by_far = top_near(), top_far()
    for h in range(HEADS):
        at_h = slice(h * DH, (h + 1) * DH)
        for part, near, out in ((0, keys_ref, fkeys_ref), (1, vals_ref, fvals_ref)):
            for d in (2, 3):
                at = (d - 2) * 32
                out[h, at : at + 16] = far_ref[z ^ d, part, :, at_h]
                out[h, at + 16 : at + 32] = faro_ref[z ^ d, part, :, at_h]
            for d in range(4, 8):
                at = 64 + (d - 4) * 16
                low, high = far_ref[z ^ d, part, :, at_h], faro_ref[z ^ d, part, :, at_h]
                out[h, at : at + 16] = jnp.concatenate([low[0:8], high[0:8]], axis=0)
            top = dot(by_near, near[h, 384:576], NN) + dot(by_far, out[h, 0:128], NN)
            out[h, 128:192] = top.astype(BF)
        scores = dot(qkv_ref[0, :, at_h], fkeys_ref[h], NT)
        first = max_ref[h]
        highest = jnp.maximum(first, jnp.max(scores, axis=1, keepdims=True))
        e = jnp.exp2((scores - highest) * (SCALE * LOG2E))
        kept = jnp.exp2((first - highest) * (SCALE * LOG2E))
        inverse = 1.0 / (kept * sum_ref[h] + jnp.sum(e, axis=1, keepdims=True))
        e = e.astype(BF)
        exps_ref[h] = e
        rnear_ref[h] = kept * inverse
        rfar_ref[h] = inverse
        att = part_ref[:, at_h] * (kept * inverse) + dot(e, fvals_ref[h], NN) * inverse
        att_ref[:, at_h] = att.astype(BF)
        attt_ref[at_h, :] = att.T.astype(BF)


def wgrad_kernel(attt_ref, og0_ref, og1_ref, og2_ref, og3_ref, mine_ref, theirs_ref):
    c, me = lax.axis_index("core"), lax.axis_index("head")
    for shift, og_ref in enumerate((og0_ref, og1_ref, og2_ref, og3_ref)):
        j = (me + shift) & 3
        r = dot(attt_ref[...], og_ref[...], NN).astype(BF)
        for i in range(4):
            for t in range(2):
                lo = r[i * 128 : (i + 1) * 128, t * 256 : t * 256 + 128]
                hi = r[i * 128 : (i + 1) * 128, t * 256 + 128 : t * 256 + 256]
                mine_ref[i, 2 * j + t] = jnp.where(c == 0, lo, hi)
                theirs_ref[i, 2 * j + t] = jnp.where(c == 0, hi, lo)


def proj_kernel(
    _, att_ref, w_hbm, og0_ref, og1_ref, og2_ref, og3_ref,
    mix0_ref, mix1_ref, mix2_ref, mix3_ref, gatt_ref, w_ref, sems,
):
    me = lax.axis_index("head")
    copies = []
    for shift in range(4):
        at = pl.multiple_of(((me + shift) & 3) * 512, 512)
        copies.append(
            pltpu.make_async_copy(w_hbm.at[:, pl.ds(at, 512)], w_ref.at[shift], sems.at[shift])
        )
    for copy in copies:
        copy.start()
    total = None
    outs = (mix0_ref, mix1_ref, mix2_ref, mix3_ref)
    for shift, og_ref in enumerate((og0_ref, og1_ref, og2_ref, og3_ref)):
        copies[shift].wait()
        w = w_ref[shift]
        outs[shift][...] = dot(att_ref[...], w, NN).astype(BF)
        term = dot(og_ref[...], w, NT)
        total = term if shift == 0 else total + term
    gatt_ref[...] = total.astype(BF)


def route_kernel(mine_ref, got_ref, own_ref, up_ref, down_ref, across_ref):
    me = lax.axis_index("dp")
    for shift, out in ((0, own_ref), (1, up_ref), (3, down_ref), (2, across_ref)):
        i = (me + shift) & 3
        out[...] = (mine_ref[i].astype(F32) + got_ref[i].astype(F32)).astype(BF)


def bwd_kernel(
    _, qkv_ref, da_ref, att_ref, exps_ref, fexps_ref, keys_ref, vals_ref, fkeys_ref, fvals_ref,
    rnear_ref, rfar_ref,
    dq_ref, mid_ref, edge_ref, own_ref, cross_ref, minec_ref, gk_ref, gv_ref,
):
    c = lax.axis_index("core")
    by_near, by_far = top_near(), top_far()
    for h in range(HEADS):
        at_h = slice(h * DH, (h + 1) * DH)
        q, da = qkv_ref[0, :, at_h], da_ref[:, at_h]
        att = att_ref[:, at_h].astype(F32)
        delta = jnp.sum(da.astype(F32) * att, axis=1, keepdims=True)
        p = fexps_ref[h].astype(F32) * rfar_ref[h]
        pgrad = dot(da, fvals_ref[h], NT)
        sgrad = (p * ((pgrad - delta) * SCALE)).astype(BF)
        dq = dot(sgrad, fkeys_ref[h], NN)
        fgk, fgv = dot(sgrad, q, TN), dot(p.astype(BF), da, TN)
        gk, gv = gk_ref.at[h], gv_ref.at[h]
        gk[576:704] = jnp.zeros((128, DH), F32)
        gv[576:704] = jnp.zeros((128, DH), F32)
        for n in range(2):
            rows = slice(n * NR, (n + 1) * NR)
            span = slice(n * NR, n * NR + JOINT)
            p = exps_ref[h, n].astype(F32) * rnear_ref[h, rows]
            pgrad = dot(da[rows], vals_ref[h, span], NT)
            sgrad = (p * ((pgrad - delta[rows]) * SCALE)).astype(BF)
            p = p.astype(BF)
            dq_ref[rows, at_h] = (dq[rows] + dot(sgrad, keys_ref[h, span], NN)).astype(BF)
            if n == 0:
                gk[0:576] = dot(sgrad, q[rows], TN)
                gv[0:576] = dot(p, da[rows], TN)
            else:
                gk[128:704] += dot(sgrad, q[rows], TN)
                gv[128:704] += dot(p, da[rows], TN)
        for part, g, f in ((0, gk, fgk), (1, gv, fgv)):
            high = f[128:192]
            hi = high.astype(BF)
            lo = (high - hi.astype(F32)).astype(BF)
            near = g[384:576] + dot(by_near, hi, TN) + dot(by_near, lo, TN)
            far = f[0:128] + dot(by_far, hi, TN) + dot(by_far, lo, TN)
            before, after = g[0:128].astype(BF), g[576:704].astype(BF)
            edge_ref[part, :, at_h] = jnp.where(c == 0, before, after)
            cross_ref[part, 160:288, at_h] = jnp.where(c == 0, after, before)
            mid_ref[part, :, at_h] = g[128:384]
            own_ref[part, :, at_h] = near[0:64]
            cross_ref[part, 0:64, at_h] = near[64:128].astype(BF)
            cross_ref[part, 64:96, at_h] = near[160:192].astype(BF)
            minec_ref[part, 0:32, at_h] = near[128:160]
            for d in (2, 3):
                at, to = (d - 2) * 32, 32 + (d - 2) * 16
                minec_ref[part, to : to + 16, at_h] = far[at : at + 16]
                cross_ref[part, 64 + to : 64 + to + 16, at_h] = far[at + 16 : at + 32].astype(BF)
            for d in (4, 6):
                at, to = 64 + (d - 4) * 16, 64 + (d - 4) * 8
                minec_ref[part, to : to + 8, at_h] = far[at : at + 8]
                minec_ref[part, to + 8 : to + 16, at_h] = far[at + 16 : at + 24]
                both = jnp.concatenate([far[at + 8 : at + 16], far[at + 24 : at + 32]], axis=0)
                cross_ref[part, 64 + to : 64 + to + 16, at_h] = both.astype(BF)


def merge_kernel(_, wsum_ref, minec_ref, got_ref, near_ref, out_ref):
    z = lax.axis_index("z")
    out_ref[:, 0:128] = wsum_ref[...]
    none = jnp.zeros((128, 128), BF)
    out_ref[z, 128:256] = none
    out_ref[z ^ 1, 128:256] = none
    for part in range(2):
        total = (minec_ref[part] + got_ref[part, 64:160].astype(F32)).astype(BF)
        near_ref[part] = total[0:32]
        low = total[64:96]
        for d in range(2, 8):
            if d < 4:
                piece = total[32 + (d - 2) * 16 : 48 + (d - 2) * 16]
            else:
                piece = low[(d - 4) * 8 : (d - 4) * 8 + 8]
                piece = jnp.concatenate([piece, jnp.zeros((8, WIDTH), BF)], axis=0)
            for col in range(4):
                at = 128 + part * 64 + col * 16
                out_ref[z ^ d, at : at + 16] = piece[:, col * 128 : (col + 1) * 128]


def sum_kernel(a_ref, b_ref, c_ref, d_ref, out_ref):
    total = a_ref[...].astype(F32) + b_ref[...].astype(F32)
    total = total + c_ref[...].astype(F32) + d_ref[...].astype(F32)
    out_ref[...] = total.astype(BF)


def sum8_kernel(a_ref, out_ref):
    total = a_ref[0, 0:128].astype(F32)
    for j in range(1, 8):
        total = total + a_ref[j, 0:128].astype(F32)
    for i in range(4):
        out_ref[i] = total.astype(BF)


def final_kernel(
    mid_ref, own_ref, got_ref, near_ref, far_ref, edge_ref, _, __,
    gk_ref, gv_ref,
):
    z, c = lax.axis_index("z"), lax.axis_index("core")
    m = pool_matrix(128, ROWS, flip=True)
    for part, out in ((0, gk_ref), (1, gv_ref)):
        l0 = own_ref[part] + got_ref[part, 0:64].astype(F32)
        l1 = near_ref[part].astype(F32)
        base = 128 + part * 64
        far = [far_ref[z ^ d, base : base + 64].astype(F32) for d in range(2, 8)]
        l2, l3 = far[0] + far[1], far[2] + far[3] + far[4] + far[5]
        l2 = jnp.concatenate([l2[i * 16 : (i + 1) * 16] for i in range(4)], axis=1)
        l3 = jnp.concatenate([l3[i * 16 : (i + 1) * 16] for i in range(4)], axis=1)
        stack = jnp.concatenate([l0, l1, l2, l3], axis=0)
        hi = stack.astype(BF)
        lo = (stack - hi.astype(F32)).astype(BF)
        spread = dot(m, hi, NN) + dot(m, lo, NN)
        total = mid_ref[part] + spread
        beside, across = got_ref[part, 160:288].astype(F32), edge_ref[part].astype(F32)
        out[0:128] = (total[0:128] + jnp.where(c == 0, across, beside)).astype(BF)
        out[128:256] = (total[128:256] + jnp.where(c == 0, beside, across)).astype(BF)


def sds(shape, dtype):
    return jax.ShapeDtypeStruct(shape, dtype)


HBM = pl.BlockSpec(memory_space=pltpu.HBM)
VMEM = pl.BlockSpec(memory_space=pltpu.VMEM)
AFTER = pl.BlockSpec(memory_space=pl.ANY)


def call(kernel, operands, outs, scratch=(), us=1, limit=LIMIT):
    return pl.pallas_call(
        kernel,
        out_shape=outs,
        in_specs=[spec for spec, _ in operands],
        out_specs=[VMEM] * len(outs),
        scratch_shapes=list(scratch),
        compiler_params=pltpu.CompilerParams(vmem_limit_bytes=limit),
        cost_estimate=pl.CostEstimate(flops=us * 10**9, bytes_accessed=1, transcendentals=0),
    )(*[array for _, array in operands])


def here(*arrays):
    return [(VMEM, array) for array in arrays]


def permute(x, axis, move):
    size = lax.axis_size(axis)
    return lax.ppermute(x, axis, [(i, move(i) % size) for i in range(size)])


def body(queries, keys, values, out_weight, out_grad):
    q, k, v = (x.reshape(ROWS, WIDTH) for x in (queries, keys, values))
    n_seq = 2 * lax.axis_size("z")
    pairs = [(i, i + 1) for i in range(1, n_seq - 1, 2)]
    pairs += [(j, i) for i, j in pairs]
    outer = functools.partial(lax.ppermute, axis_name=("z", "core"), perm=pairs)
    swap = functools.partial(permute, axis="core", move=lambda i: i ^ 1)
    hop = functools.partial(permute, axis="z", move=lambda i: i ^ 1)
    dma = pltpu.SemaphoreType.DMA

    og = out_grad.reshape(ROWS, WIDTH)

    qkv, chip, near, far, edge = call(
        prep_kernel, [(HBM, q), (HBM, k), (HBM, v)],
        [sds((3, ROWS, WIDTH), BF), sds((2, 192, WIDTH), BF), sds((2, 32, WIDTH), BF),
         sds((8, 2, 16, WIDTH), BF), sds((2, NR, WIDTH), BF)],
        [dma((3,))], limit=62 * 1024 * 1024,
    )
    sib = swap(chip)
    near_got = hop(near)
    near_other = swap(near_got)
    edge_got = outer(edge)
    far_got = lax.all_to_all(far, "z", 0, 0)
    far_other = swap(far_got)
    ogs = [og] + [permute(og, "head", lambda i, m=m: i - m) for m in (1, 2, 3)]

    (token,) = call(token_kernel, [(AFTER, x) for x in ogs[1:]], [sds((8, 128), F32)], us=10)

    column = sds((HEADS, ROWS, 1), F32)
    keys_near, vals_near, exps, part, top, total = call(
        near_kernel, [(AFTER, token)] + here(qkv, edge_got, chip, sib, near_got, near_other),
        [sds((HEADS, NEAR, DH), BF), sds((HEADS, NEAR, DH), BF), sds((HEADS, 2, NR, JOINT), BF),
         sds((ROWS, WIDTH), F32), column, column],
        us=20,
    )
    att, attt, far_exps, keys_far, vals_far, rnear, rfar = call(
        far_kernel, here(qkv, far_got, far_other, keys_near, vals_near, part, top, total),
        [sds((ROWS, WIDTH), BF), sds((WIDTH, ROWS), BF), sds((HEADS, ROWS, FAR), BF),
         sds((HEADS, FAR, DH), BF), sds((HEADS, FAR, DH), BF), column, column],
    )
    mine, theirs = call(wgrad_kernel, here(attt, *ogs), [sds((4, 8, 128, 128), BF)] * 2)
    got = swap(theirs)
    *mixes, gatt = call(
        proj_kernel, [(AFTER, mine), (VMEM, att), (HBM, out_weight)] + here(*ogs),
        [sds((ROWS, WIDTH), BF)] * 5, [pltpu.VMEM((4, WIDTH, 512), BF), dma((4,))],
    )
    mix_parts = [mixes[0]]
    mix_parts += [permute(mixes[m], "head", lambda i, m=m: i + m) for m in (1, 2, 3)]

    kept, to_up, to_down, to_across = call(
        route_kernel, here(mine, got), [sds((8, 128, 128), BF)] * 4
    )
    from_down = permute(to_up, "dp", lambda i: i + 1)
    from_up = permute(to_down, "dp", lambda i: i - 1)
    from_across = permute(to_across, "dp", lambda i: i + 2)

    dq, mid, edge_grad, own_grad, cross, minec = call(
        bwd_kernel,
        [(AFTER, kept)]
        + here(qkv, gatt, att, exps, far_exps, keys_near, vals_near, keys_far, vals_far)
        + here(rnear, rfar),
        [sds((ROWS, WIDTH), BF), sds((2, ROWS, WIDTH), F32), sds((2, NR, WIDTH), BF),
         sds((2, 64, WIDTH), F32), sds((2, 288, WIDTH), BF),
         sds((2, 96, WIDTH), F32)],
        [pltpu.VMEM((HEADS, NEAR, DH), F32)] * 2, us=20,
    )
    cross_got = swap(cross)
    edge_back = outer(edge_grad)
    (wsum,) = call(
        sum_kernel, here(kept, from_down, from_up, from_across), [sds((8, 128, 128), BF)], us=8
    )
    near_grad, both = call(
        merge_kernel, [(AFTER, edge_back)] + here(wsum, minec, cross_got),
        [sds((2, 32, WIDTH), BF), sds((8, 256, 128), BF)],
    )
    near_back = hop(near_grad)
    both_got = lax.all_to_all(both, "z", 0, 0)
    (mixed,) = call(sum_kernel, here(*mix_parts), [sds((ROWS, WIDTH), BF)])
    (wpart,) = call(
        sum8_kernel, here(both_got), [sds((4, 128, 128), BF)], us=20
    )
    wall = lax.all_to_all(wpart, "dp", 0, 0)
    grad_out_weight = wall.reshape(WIDTH, 128).astype(F32)

    grad_keys, grad_values = call(
        final_kernel,
        here(mid, own_grad, cross_got, near_back, both_got, edge_back)
        + [(AFTER, wpart), (AFTER, mixed)],
        [sds((ROWS, WIDTH), BF)] * 2,
    )
    shape = (1, ROWS, WIDTH)
    return (
        mixed.reshape(shape), dq.reshape(shape), grad_keys.reshape(shape),
        grad_values.reshape(shape), grad_out_weight,
    )


def solution(mesh):
    dp, seq, head = (mesh.shape[name] for name in ("dp", "seq", "head"))
    cut = Mesh(mesh.devices.reshape(dp, seq // 2, 2, head), ("dp", "z", "core", "head"))
    rows = P("dp", ("z", "core"), "head")
    return jax.shard_map(
        body,
        mesh=cut,
        in_specs=(rows, rows, rows, P("head", None), rows),
        out_specs=(rows, rows, rows, rows, P("head", ("z", "core"))),
        check_vma=False,
    )
```

```python
import functools
import math

import jax
import jax.numpy as jnp
from jax import lax
from jax.experimental import pallas as pl
from jax.experimental.pallas import tpu as pltpu
from jax.sharding import Mesh, PartitionSpec as P

DH = 128
NR = 128
C = 64
HEADS = 4
ROWS = 256
WIDTH = 512
NEAR = 704
JOINT = 576
FAR = 192
BF = jnp.bfloat16
F32 = jnp.float32
LIMIT = 36 * 1024 * 1024
SCALE = 1.0 / math.sqrt(DH)
LOG2E = math.log2(math.e)


def pool_matrix(rows, positions, flip=False):
    shape = (positions, rows) if flip else (rows, positions)
    r = lax.broadcasted_iota(jnp.int32, shape, 1 if flip else 0)
    p = lax.broadcasted_iota(jnp.int32, shape, 0 if flip else 1)
    l0 = (r < 64) & ((p >> 2) == r)
    l1 = (r >= 64) & (r < 96) & ((p >> 3) == r - 64)
    l2 = (r >= 96) & (r < 112) & ((p >> 4) == r - 96)
    l3 = (r >= 112) & (r < 120) & ((p >> 5) == r - 112)
    out = jnp.where(l0, 0.25, 0.0) + jnp.where(l1, 0.125, 0.0)
    out = out + jnp.where(l2, 0.0625, 0.0) + jnp.where(l3, 0.03125, 0.0)
    return out.astype(BF)


def top_near():
    r = lax.broadcasted_iota(jnp.int32, (64, 192), 0)
    j = lax.broadcasted_iota(jnp.int32, (64, 192), 1)
    l0 = (j < 128) & ((j >> 4) == r)
    l1 = (j >= 128) & (8 + ((j - 128) >> 3) == r)
    return (jnp.where(l0, 0.0625, 0.0) + jnp.where(l1, 0.125, 0.0)).astype(BF)


def top_far():
    r = lax.broadcasted_iota(jnp.int32, (64, 128), 0)
    j = lax.broadcasted_iota(jnp.int32, (64, 128), 1)
    l2 = (j < 64) & (16 + (j >> 2) == r)
    l3 = (j >= 64) & (32 + ((j - 64) >> 1) == r)
    return (jnp.where(l2, 0.25, 0.0) + jnp.where(l3, 0.5, 0.0)).astype(BF)


def dot(a, b, dims):
    return lax.dot_general(a, b, (dims, ((), ())), preferred_element_type=F32)


NN = ((1,), (0,))
NT = ((1,), (1,))
TN = ((0,), (0,))


def prep_kernel(k_hbm, v_hbm, chip_ref, near_ref, far_ref, edge_ref, held, sems):
    z, c = lax.axis_index("z"), lax.axis_index("core")
    copies = [
        pltpu.make_async_copy(src, held.at[at], sems.at[at])
        for at, src in ((0, k_hbm), (1, v_hbm))
    ]
    for copy in copies:
        copy.start()
    m = pool_matrix(128, ROWS)
    for part in range(2):
        copies[part].wait()
        x = held[part]
        pooled = dot(m, x, NN).astype(BF)
        chip_ref[part, 0:64] = pooled[0:64]
        near_ref[part] = pooled[64:96]
        for d in range(8):
            far_ref[z ^ d, part] = pooled[112:128] if d >= 4 else pooled[96:112]
        chip_ref[part, 64:192] = jnp.where(c == 0, x[NR:], x[:NR])
        edge_ref[part] = jnp.where(c == 0, x[:NR], x[NR:])


def token_kernel(_, __, ___, out_ref):
    out_ref[...] = jnp.zeros_like(out_ref)


def near_kernel(
    _, q_ref, k_ref, v_ref, edge_ref, chip_ref, sib_ref, near_ref, nearo_ref,
    keys_ref, vals_ref, exps_ref, part_ref, max_ref, sum_ref,
):
    z, c = lax.axis_index("z"), lax.axis_index("core")
    s = z * 2 + c
    col = lax.broadcasted_iota(jnp.int32, (1, JOINT), 1)
    for h in range(HEADS):
        at_h = slice(h * DH, (h + 1) * DH)
        for part, own_ref, out in ((0, k_ref, keys_ref), (1, v_ref, vals_ref)):
            beside, across = sib_ref[part, 64:192, at_h], edge_ref[part, :, at_h]
            out[h, 0:128] = jnp.where(c == 0, across, beside)
            out[h, 128:384] = own_ref[:, at_h]
            out[h, 384:448] = chip_ref[part, 0:64, at_h]
            out[h, 448:512] = sib_ref[part, 0:64, at_h]
            out[h, 512:544] = near_ref[part, :, at_h]
            out[h, 544:576] = nearo_ref[part, :, at_h]
            out[h, 576:704] = jnp.where(c == 0, beside, across)
        for n in range(2):
            rows = slice(n * NR, (n + 1) * NR)
            span = slice(n * NR, n * NR + JOINT)
            scores = dot(q_ref[rows, at_h], keys_ref[h, span], NT)
            if n == 0:
                hidden = (col < NR) & (s == 0)
            else:
                hidden = (col >= JOINT - NR) & (s == 15)
            scores = jnp.where(hidden, -jnp.inf, scores)
            highest = jnp.max(scores, axis=1, keepdims=True)
            e = jnp.exp2((scores - highest) * (SCALE * LOG2E))
            max_ref[h, rows] = highest
            sum_ref[h, rows] = jnp.sum(e, axis=1, keepdims=True)
            e = e.astype(BF)
            exps_ref[h, n] = e
            part_ref[rows, at_h] = dot(e, vals_ref[h, span], NN)


def far_kernel(
    q_ref, far_ref, faro_ref, keys_ref, vals_ref, part_ref, max_ref, sum_ref,
    att_ref, attt_ref, exps_ref, fkeys_ref, fvals_ref, rnear_ref, rfar_ref,
):
    z = lax.axis_index("z")
    by_near, by_far = top_near(), top_far()
    for h in range(HEADS):
        at_h = slice(h * DH, (h + 1) * DH)
        for part, near, out in ((0, keys_ref, fkeys_ref), (1, vals_ref, fvals_ref)):
            for d in (2, 3):
                at = (d - 2) * 32
                out[h, at : at + 16] = far_ref[z ^ d, part, :, at_h]
                out[h, at + 16 : at + 32] = faro_ref[z ^ d, part, :, at_h]
            for d in range(4, 8):
                at = 64 + (d - 4) * 16
                low, high = far_ref[z ^ d, part, :, at_h], faro_ref[z ^ d, part, :, at_h]
                out[h, at : at + 16] = jnp.concatenate([low[0:8], high[0:8]], axis=0)
            top = dot(by_near, near[h, 384:576], NN) + dot(by_far, out[h, 0:128], NN)
            out[h, 128:192] = top.astype(BF)
        scores = dot(q_ref[:, at_h], fkeys_ref[h], NT)
        first = max_ref[h]
        highest = jnp.maximum(first, jnp.max(scores, axis=1, keepdims=True))
        e = jnp.exp2((scores - highest) * (SCALE * LOG2E))
        kept = jnp.exp2((first - highest) * (SCALE * LOG2E))
        inverse = 1.0 / (kept * sum_ref[h] + jnp.sum(e, axis=1, keepdims=True))
        e = e.astype(BF)
        exps_ref[h] = e
        rnear_ref[h] = kept * inverse
        rfar_ref[h] = inverse
        att = part_ref[:, at_h] * (kept * inverse) + dot(e, fvals_ref[h], NN) * inverse
        att_ref[:, at_h] = att.astype(BF)
        attt_ref[at_h, :] = att.T.astype(BF)


def wgrad_kernel(attt_ref, og0_ref, og1_ref, og2_ref, og3_ref, mine_ref, theirs_ref):
    c, me = lax.axis_index("core"), lax.axis_index("head")
    for shift, og_ref in enumerate((og0_ref, og1_ref, og2_ref, og3_ref)):
        j = (me + shift) & 3
        r = dot(attt_ref[...], og_ref[...], NN).astype(BF)
        for i in range(4):
            for t in range(2):
                lo = r[i * 128 : (i + 1) * 128, t * 256 : t * 256 + 128]
                hi = r[i * 128 : (i + 1) * 128, t * 256 + 128 : t * 256 + 256]
                mine_ref[i, 2 * j + t] = jnp.where(c == 0, lo, hi)
                theirs_ref[i, 2 * j + t] = jnp.where(c == 0, hi, lo)


def proj_kernel(
    _, att_ref, w_hbm, og0_ref, og1_ref, og2_ref, og3_ref,
    mix0_ref, mix1_ref, mix2_ref, mix3_ref, gatt_ref, w_ref, sems,
):
    me = lax.axis_index("head")
    copies = []
    for shift in range(4):
        at = pl.multiple_of(((me + shift) & 3) * 512, 512)
        copies.append(
            pltpu.make_async_copy(w_hbm.at[:, pl.ds(at, 512)], w_ref.at[shift], sems.at[shift])
        )
    for copy in copies:
        copy.start()
    total = None
    outs = (mix0_ref, mix1_ref, mix2_ref, mix3_ref)
    for shift, og_ref in enumerate((og0_ref, og1_ref, og2_ref, og3_ref)):
        copies[shift].wait()
        w = w_ref[shift]
        outs[shift][...] = dot(att_ref[...], w, NN).astype(BF)
        term = dot(og_ref[...], w, NT)
        total = term if shift == 0 else total + term
    gatt_ref[...] = total.astype(BF)


def route_kernel(mine_ref, got_ref, own_ref, up_ref, down_ref, across_ref):
    me = lax.axis_index("dp")
    for shift, out in ((0, own_ref), (1, up_ref), (3, down_ref), (2, across_ref)):
        i = (me + shift) & 3
        out[...] = (mine_ref[i].astype(F32) + got_ref[i].astype(F32)).astype(BF)


def bwd_kernel(
    _, q_ref, da_ref, att_ref, exps_ref, fexps_ref, keys_ref, vals_ref, fkeys_ref, fvals_ref,
    rnear_ref, rfar_ref,
    dq_ref, mid_ref, edge_ref, own_ref, cross_ref, minec_ref, gk_ref, gv_ref,
):
    c = lax.axis_index("core")
    by_near, by_far = top_near(), top_far()
    for h in range(HEADS):
        at_h = slice(h * DH, (h + 1) * DH)
        q, da = q_ref[:, at_h], da_ref[:, at_h]
        att = att_ref[:, at_h].astype(F32)
        delta = jnp.sum(da.astype(F32) * att, axis=1, keepdims=True)
        p = fexps_ref[h].astype(F32) * rfar_ref[h]
        pgrad = dot(da, fvals_ref[h], NT)
        sgrad = (p * ((pgrad - delta) * SCALE)).astype(BF)
        dq = dot(sgrad, fkeys_ref[h], NN)
        fgk, fgv = dot(sgrad, q, TN), dot(p.astype(BF), da, TN)
        gk, gv = gk_ref.at[h], gv_ref.at[h]
        gk[576:704] = jnp.zeros((128, DH), F32)
        gv[576:704] = jnp.zeros((128, DH), F32)
        for n in range(2):
            rows = slice(n * NR, (n + 1) * NR)
            span = slice(n * NR, n * NR + JOINT)
            p = exps_ref[h, n].astype(F32) * rnear_ref[h, rows]
            pgrad = dot(da[rows], vals_ref[h, span], NT)
            sgrad = (p * ((pgrad - delta[rows]) * SCALE)).astype(BF)
            p = p.astype(BF)
            dq_ref[rows, at_h] = (dq[rows] + dot(sgrad, keys_ref[h, span], NN)).astype(BF)
            if n == 0:
                gk[0:576] = dot(sgrad, q[rows], TN)
                gv[0:576] = dot(p, da[rows], TN)
            else:
                gk[128:704] += dot(sgrad, q[rows], TN)
                gv[128:704] += dot(p, da[rows], TN)
        for part, g, f in ((0, gk, fgk), (1, gv, fgv)):
            high = f[128:192]
            hi = high.astype(BF)
            lo = (high - hi.astype(F32)).astype(BF)
            near = g[384:576] + dot(by_near, hi, TN) + dot(by_near, lo, TN)
            far = f[0:128] + dot(by_far, hi, TN) + dot(by_far, lo, TN)
            before, after = g[0:128].astype(BF), g[576:704].astype(BF)
            edge_ref[part, :, at_h] = jnp.where(c == 0, before, after)
            cross_ref[part, 160:288, at_h] = jnp.where(c == 0, after, before)
            mid_ref[part, :, at_h] = g[128:384]
            own_ref[part, :, at_h] = near[0:64]
            cross_ref[part, 0:64, at_h] = near[64:128].astype(BF)
            cross_ref[part, 64:96, at_h] = near[160:192].astype(BF)
            minec_ref[part, 0:32, at_h] = near[128:160]
            for d in (2, 3):
                at, to = (d - 2) * 32, 32 + (d - 2) * 16
                minec_ref[part, to : to + 16, at_h] = far[at : at + 16]
                cross_ref[part, 64 + to : 64 + to + 16, at_h] = far[at + 16 : at + 32].astype(BF)
            for d in (4, 6):
                at, to = 64 + (d - 4) * 16, 64 + (d - 4) * 8
                minec_ref[part, to : to + 8, at_h] = far[at : at + 8]
                minec_ref[part, to + 8 : to + 16, at_h] = far[at + 16 : at + 24]
                both = jnp.concatenate([far[at + 8 : at + 16], far[at + 24 : at + 32]], axis=0)
                cross_ref[part, 64 + to : 64 + to + 16, at_h] = both.astype(BF)


def merge_kernel(_, wsum_ref, minec_ref, got_ref, near_ref, out_ref):
    z = lax.axis_index("z")
    out_ref[:, 0:128] = wsum_ref[...]
    none = jnp.zeros((128, 128), BF)
    out_ref[z, 128:256] = none
    out_ref[z ^ 1, 128:256] = none
    for part in range(2):
        total = (minec_ref[part] + got_ref[part, 64:160].astype(F32)).astype(BF)
        near_ref[part] = total[0:32]
        low = total[64:96]
        for d in range(2, 8):
            if d < 4:
                piece = total[32 + (d - 2) * 16 : 48 + (d - 2) * 16]
            else:
                piece = low[(d - 4) * 8 : (d - 4) * 8 + 8]
                piece = jnp.concatenate([piece, jnp.zeros((8, WIDTH), BF)], axis=0)
            for col in range(4):
                at = 128 + part * 64 + col * 16
                out_ref[z ^ d, at : at + 16] = piece[:, col * 128 : (col + 1) * 128]


def sum_kernel(a_ref, b_ref, c_ref, d_ref, out_ref):
    total = a_ref[...].astype(F32) + b_ref[...].astype(F32)
    total = total + c_ref[...].astype(F32) + d_ref[...].astype(F32)
    out_ref[...] = total.astype(BF)


def mixed_kernel(a_ref, b_ref, c_ref, d_ref, out_ref, token_ref):
    sum_kernel(a_ref, b_ref, c_ref, d_ref, out_ref)
    token_ref[...] = jnp.zeros_like(token_ref)


def sum8_kernel(a_ref, out_ref):
    total = a_ref[0, 0:128].astype(F32)
    for j in range(1, 8):
        total = total + a_ref[j, 0:128].astype(F32)
    out_ref[...] = total.astype(BF)


def collect_kernel(_, __, a_ref, b_ref, c_ref, d_ref, out_ref):
    me = lax.axis_index("dp")
    for shift, ref in ((0, a_ref), (1, b_ref), (2, c_ref), (3, d_ref)):
        out_ref[(me + shift) & 3] = ref[...].astype(F32)


def final_kernel(
    mid_ref, own_ref, got_ref, near_ref, far_ref, edge_ref, _,
    gk_ref, gv_ref, token_ref,
):
    z, c = lax.axis_index("z"), lax.axis_index("core")
    m = pool_matrix(128, ROWS, flip=True)
    for part, out in ((0, gk_ref), (1, gv_ref)):
        l0 = own_ref[part] + got_ref[part, 0:64].astype(F32)
        l1 = near_ref[part].astype(F32)
        base = 128 + part * 64
        far = [far_ref[z ^ d, base : base + 64].astype(F32) for d in range(2, 8)]
        l2, l3 = far[0] + far[1], far[2] + far[3] + far[4] + far[5]
        l2 = jnp.concatenate([l2[i * 16 : (i + 1) * 16] for i in range(4)], axis=1)
        l3 = jnp.concatenate([l3[i * 16 : (i + 1) * 16] for i in range(4)], axis=1)
        stack = jnp.concatenate([l0, l1, l2, l3], axis=0)
        hi = stack.astype(BF)
        lo = (stack - hi.astype(F32)).astype(BF)
        spread = dot(m, hi, NN) + dot(m, lo, NN)
        total = mid_ref[part] + spread
        beside, across = got_ref[part, 160:288].astype(F32), edge_ref[part].astype(F32)
        out[0:128] = (total[0:128] + jnp.where(c == 0, across, beside)).astype(BF)
        out[128:256] = (total[128:256] + jnp.where(c == 0, beside, across)).astype(BF)
    token_ref[...] = jnp.zeros_like(token_ref)


def sds(shape, dtype):
    return jax.ShapeDtypeStruct(shape, dtype)


TOKEN = sds((8, 128), F32)


HBM = pl.BlockSpec(memory_space=pltpu.HBM)
VMEM = pl.BlockSpec(memory_space=pltpu.VMEM)
AFTER = pl.BlockSpec(memory_space=pl.ANY)


def call(kernel, operands, outs, scratch=(), us=1, limit=LIMIT):
    return pl.pallas_call(
        kernel,
        out_shape=outs,
        in_specs=[spec for spec, _ in operands],
        out_specs=[VMEM] * len(outs),
        scratch_shapes=list(scratch),
        compiler_params=pltpu.CompilerParams(vmem_limit_bytes=limit),
        cost_estimate=pl.CostEstimate(flops=us * 10**9, bytes_accessed=1, transcendentals=0),
    )(*[array for _, array in operands])


def here(*arrays):
    return [(VMEM, array) for array in arrays]


def permute(x, axis, move):
    size = lax.axis_size(axis)
    return lax.ppermute(x, axis, [(i, move(i) % size) for i in range(size)])


def body(queries, keys, values, out_weight, out_grad):
    q, k, v = (x.reshape(ROWS, WIDTH) for x in (queries, keys, values))
    n_seq = 2 * lax.axis_size("z")
    pairs = [(i, i + 1) for i in range(1, n_seq - 1, 2)]
    pairs += [(j, i) for i, j in pairs]
    outer = functools.partial(lax.ppermute, axis_name=("z", "core"), perm=pairs)
    swap = functools.partial(permute, axis="core", move=lambda i: i ^ 1)
    hop = functools.partial(permute, axis="z", move=lambda i: i ^ 1)
    dma = pltpu.SemaphoreType.DMA

    og = out_grad.reshape(ROWS, WIDTH)

    chip, near, far, edge = call(
        prep_kernel, [(HBM, k), (HBM, v)],
        [sds((2, 192, WIDTH), BF), sds((2, 32, WIDTH), BF), sds((8, 2, 16, WIDTH), BF),
         sds((2, NR, WIDTH), BF)],
        [pltpu.VMEM((2, ROWS, WIDTH), BF), dma((2,))], limit=62 * 1024 * 1024,
    )
    sib = swap(chip)
    near_got = hop(near)
    near_other = swap(near_got)
    edge_got = outer(edge)
    far_got = lax.all_to_all(far, "z", 0, 0)
    far_other = swap(far_got)
    ogs = [og] + [permute(og, "head", lambda i, m=m: i - m) for m in (1, 2, 3)]

    (token,) = call(token_kernel, [(AFTER, x) for x in ogs[1:]], [sds((8, 128), F32)], us=10)

    column = sds((HEADS, ROWS, 1), F32)
    keys_near, vals_near, exps, part, top, total = call(
        near_kernel, [(AFTER, token)] + here(q, k, v, edge_got, chip, sib, near_got, near_other),
        [sds((HEADS, NEAR, DH), BF), sds((HEADS, NEAR, DH), BF), sds((HEADS, 2, NR, JOINT), BF),
         sds((ROWS, WIDTH), F32), column, column],
        us=20,
    )
    att, attt, far_exps, keys_far, vals_far, rnear, rfar = call(
        far_kernel, here(q, far_got, far_other, keys_near, vals_near, part, top, total),
        [sds((ROWS, WIDTH), BF), sds((WIDTH, ROWS), BF), sds((HEADS, ROWS, FAR), BF),
         sds((HEADS, FAR, DH), BF), sds((HEADS, FAR, DH), BF), column, column],
    )
    mine, theirs = call(wgrad_kernel, here(attt, *ogs), [sds((4, 8, 128, 128), BF)] * 2)
    got = swap(theirs)
    *mixes, gatt = call(
        proj_kernel, [(AFTER, mine), (VMEM, att), (HBM, out_weight)] + here(*ogs),
        [sds((ROWS, WIDTH), BF)] * 5, [pltpu.VMEM((4, WIDTH, 512), BF), dma((4,))],
    )
    mix_parts = [mixes[0]]
    mix_parts += [permute(mixes[m], "head", lambda i, m=m: i + m) for m in (2, 1, 3)]

    kept, to_up, to_down, to_across = call(
        route_kernel, here(mine, got), [sds((8, 128, 128), BF)] * 4
    )
    from_across = permute(to_across, "dp", lambda i: i + 2)
    from_down = permute(to_up, "dp", lambda i: i + 1)
    from_up = permute(to_down, "dp", lambda i: i - 1)

    dq, mid, edge_grad, own_grad, cross, minec = call(
        bwd_kernel,
        [(AFTER, kept)]
        + here(q, gatt, att, exps, far_exps, keys_near, vals_near, keys_far, vals_far)
        + here(rnear, rfar),
        [sds((ROWS, WIDTH), BF), sds((2, ROWS, WIDTH), F32), sds((2, NR, WIDTH), BF),
         sds((2, 64, WIDTH), F32), sds((2, 288, WIDTH), BF),
         sds((2, 96, WIDTH), F32)],
        [pltpu.VMEM((HEADS, NEAR, DH), F32)] * 2, us=20,
    )
    cross_got = swap(cross)
    edge_back = outer(edge_grad)
    (wsum,) = call(
        sum_kernel, here(kept, from_across, from_down, from_up), [sds((8, 128, 128), BF)], us=8
    )
    near_grad, both = call(
        merge_kernel, [(AFTER, edge_back)] + here(wsum, minec, cross_got),
        [sds((2, 32, WIDTH), BF), sds((8, 256, 128), BF)],
    )
    near_back = hop(near_grad)
    both_got = lax.all_to_all(both, "z", 0, 0)
    (wpart,) = call(
        sum8_kernel, here(both_got), [sds((128, 128), BF)], us=20
    )
    mixed, token_mixed = call(
        mixed_kernel, here(*mix_parts), [sds((ROWS, WIDTH), BF), TOKEN],
    )
    wparts = [wpart] + [permute(wpart, "dp", lambda i, m=m: i - m) for m in (1, 2, 3)]

    grad_keys, grad_values, token_keys = call(
        final_kernel,
        here(mid, own_grad, cross_got, near_back, both_got, edge_back)
        + [(AFTER, wpart)],
        [sds((ROWS, WIDTH), BF)] * 2 + [TOKEN],
    )
    (wall,) = call(
        collect_kernel, [(AFTER, token_mixed), (AFTER, token_keys)] + here(*wparts),
        [sds((4, 128, 128), F32)],
    )
    grad_out_weight = wall.reshape(WIDTH, 128)
    shape = (1, ROWS, WIDTH)
    return (
        mixed.reshape(shape), dq.reshape(shape), grad_keys.reshape(shape),
        grad_values.reshape(shape), grad_out_weight,
    )


def solution(mesh):
    dp, seq, head = (mesh.shape[name] for name in ("dp", "seq", "head"))
    cut = Mesh(mesh.devices.reshape(dp, seq // 2, 2, head), ("dp", "z", "core", "head"))
    rows = P("dp", ("z", "core"), "head")
    return jax.shard_map(
        body,
        mesh=cut,
        in_specs=(rows, rows, rows, P("head", None), rows),
        out_specs=(rows, rows, rows, rows, P("head", ("z", "core"))),
        check_vma=False,
    )
```

```python
import functools
import math

import jax
import jax.numpy as jnp
from jax import lax
from jax.experimental import pallas as pl
from jax.experimental.pallas import tpu as pltpu
from jax.sharding import Mesh, PartitionSpec as P

DH = 128
NR = 128
C = 64
HEADS = 4
ROWS = 256
WIDTH = 512
NEAR = 640
JOINT = 512
FAR = 256
BF = jnp.bfloat16
F32 = jnp.float32
LIMIT = 36 * 1024 * 1024
SCALE = 1.0 / math.sqrt(DH)
LOG2E = math.log2(math.e)


def pool_matrix(rows, positions, flip=False):
    shape = (positions, rows) if flip else (rows, positions)
    r = lax.broadcasted_iota(jnp.int32, shape, 1 if flip else 0)
    p = lax.broadcasted_iota(jnp.int32, shape, 0 if flip else 1)
    l0 = (r < 64) & ((p >> 2) == r)
    l1 = (r >= 64) & (r < 96) & ((p >> 3) == r - 64)
    l2 = (r >= 96) & (r < 112) & ((p >> 4) == r - 96)
    l3 = (r >= 112) & (r < 120) & ((p >> 5) == r - 112)
    out = jnp.where(l0, 0.25, 0.0) + jnp.where(l1, 0.125, 0.0)
    out = out + jnp.where(l2, 0.0625, 0.0) + jnp.where(l3, 0.03125, 0.0)
    return out.astype(BF)


def top_near():
    r = lax.broadcasted_iota(jnp.int32, (64, 128), 0)
    j = lax.broadcasted_iota(jnp.int32, (64, 128), 1)
    return jnp.where((j >> 4) == r, 0.0625, 0.0).astype(BF)


def top_far():
    r = lax.broadcasted_iota(jnp.int32, (64, 192), 0)
    j = lax.broadcasted_iota(jnp.int32, (64, 192), 1)
    l1 = (j < 64) & (8 + (j >> 3) == r)
    l2 = (j >= 64) & (j < 128) & (16 + ((j - 64) >> 2) == r)
    l3 = (j >= 128) & (32 + ((j - 128) >> 1) == r)
    out = jnp.where(l1, 0.125, 0.0) + jnp.where(l2, 0.25, 0.0) + jnp.where(l3, 0.5, 0.0)
    return out.astype(BF)


def dot(a, b, dims):
    return lax.dot_general(a, b, (dims, ((), ())), preferred_element_type=F32)


NN = ((1,), (0,))
NT = ((1,), (1,))
TN = ((0,), (0,))


def prep_kernel(k_hbm, v_hbm, chip_ref, near_ref, far_ref, edge_ref, held, sems):
    z, c = lax.axis_index("z"), lax.axis_index("core")
    copies = [
        pltpu.make_async_copy(src, held.at[at], sems.at[at])
        for at, src in ((0, k_hbm), (1, v_hbm))
    ]
    for copy in copies:
        copy.start()
    m = pool_matrix(128, ROWS)
    for part in range(2):
        copies[part].wait()
        x = held[part]
        pooled = dot(m, x, NN).astype(BF)
        chip_ref[part, 0:64] = pooled[0:64]
        near_ref[part] = pooled[64:96]
        for d in range(8):
            far_ref[z ^ d, part] = pooled[112:128] if d >= 4 else pooled[96:112]
        chip_ref[part, 64:192] = jnp.where(c == 0, x[NR:], x[:NR])
        edge_ref[part] = jnp.where(c == 0, x[:NR], x[NR:])


def token_kernel(_, __, ___, out_ref):
    out_ref[...] = jnp.zeros_like(out_ref)


def near_kernel(
    _, q_ref, k_ref, v_ref, edge_ref, chip_ref, sib_ref,
    keys_ref, vals_ref, exps_ref, part_ref, max_ref, sum_ref,
):
    z, c = lax.axis_index("z"), lax.axis_index("core")
    s = z * 2 + c
    col = lax.broadcasted_iota(jnp.int32, (1, JOINT), 1)
    for h in range(HEADS):
        at_h = slice(h * DH, (h + 1) * DH)
        for part, own_ref, out in ((0, k_ref, keys_ref), (1, v_ref, vals_ref)):
            beside, across = sib_ref[part, 64:192, at_h], edge_ref[part, :, at_h]
            out[h, 0:128] = jnp.where(c == 0, across, beside)
            out[h, 128:384] = own_ref[:, at_h]
            out[h, 384:448] = chip_ref[part, 0:64, at_h]
            out[h, 448:512] = sib_ref[part, 0:64, at_h]
            out[h, 512:640] = jnp.where(c == 0, beside, across)
        for n in range(2):
            rows = slice(n * NR, (n + 1) * NR)
            span = slice(n * NR, n * NR + JOINT)
            scores = dot(q_ref[rows, at_h], keys_ref[h, span], NT)
            if n == 0:
                hidden = (col < NR) & (s == 0)
            else:
                hidden = (col >= JOINT - NR) & (s == 15)
            scores = jnp.where(hidden, -jnp.inf, scores)
            highest = jnp.max(scores, axis=1, keepdims=True)
            e = jnp.exp2((scores - highest) * (SCALE * LOG2E))
            max_ref[h, rows] = highest
            sum_ref[h, rows] = jnp.sum(e, axis=1, keepdims=True)
            e = e.astype(BF)
            exps_ref[h, n] = e
            part_ref[rows, at_h] = dot(e, vals_ref[h, span], NN)


def far_kernel(
    q_ref, near_ref, nearo_ref, far_ref, faro_ref, keys_ref, vals_ref, part_ref, max_ref, sum_ref,
    att_ref, attt_ref, exps_ref, fkeys_ref, fvals_ref, rnear_ref, rfar_ref,
):
    z = lax.axis_index("z")
    by_near, by_far = top_near(), top_far()
    for h in range(HEADS):
        at_h = slice(h * DH, (h + 1) * DH)
        for part, near, out in ((0, keys_ref, fkeys_ref), (1, vals_ref, fvals_ref)):
            out[h, 0:32] = near_ref[part, :, at_h]
            out[h, 32:64] = nearo_ref[part, :, at_h]
            for d in (2, 3):
                at = 64 + (d - 2) * 32
                out[h, at : at + 16] = far_ref[z ^ d, part, :, at_h]
                out[h, at + 16 : at + 32] = faro_ref[z ^ d, part, :, at_h]
            for d in range(4, 8):
                at = 128 + (d - 4) * 16
                low, high = far_ref[z ^ d, part, :, at_h], faro_ref[z ^ d, part, :, at_h]
                out[h, at : at + 16] = jnp.concatenate([low[0:8], high[0:8]], axis=0)
            top = dot(by_near, near[h, 384:512], NN) + dot(by_far, out[h, 0:192], NN)
            out[h, 192:256] = top.astype(BF)
        scores = dot(q_ref[:, at_h], fkeys_ref[h], NT)
        first = max_ref[h]
        highest = jnp.maximum(first, jnp.max(scores, axis=1, keepdims=True))
        e = jnp.exp2((scores - highest) * (SCALE * LOG2E))
        kept = jnp.exp2((first - highest) * (SCALE * LOG2E))
        inverse = 1.0 / (kept * sum_ref[h] + jnp.sum(e, axis=1, keepdims=True))
        e = e.astype(BF)
        exps_ref[h] = e
        rnear_ref[h] = kept * inverse
        rfar_ref[h] = inverse
        att = part_ref[:, at_h] * (kept * inverse) + dot(e, fvals_ref[h], NN) * inverse
        att_ref[:, at_h] = att.astype(BF)
        attt_ref[at_h, :] = att.T.astype(BF)


def wgrad_kernel(attt_ref, og0_ref, og1_ref, og2_ref, og3_ref, mine_ref, theirs_ref):
    c, me = lax.axis_index("core"), lax.axis_index("head")
    for shift, og_ref in enumerate((og0_ref, og1_ref, og2_ref, og3_ref)):
        j = (me + shift) & 3
        r = dot(attt_ref[...], og_ref[...], NN).astype(BF)
        for i in range(4):
            for t in range(2):
                lo = r[i * 128 : (i + 1) * 128, t * 256 : t * 256 + 128]
                hi = r[i * 128 : (i + 1) * 128, t * 256 + 128 : t * 256 + 256]
                mine_ref[i, 2 * j + t] = jnp.where(c == 0, lo, hi)
                theirs_ref[i, 2 * j + t] = jnp.where(c == 0, hi, lo)


def proj_kernel(
    _, att_ref, w_hbm, og0_ref, og1_ref, og2_ref, og3_ref,
    mix0_ref, mix1_ref, mix2_ref, mix3_ref, gatt_ref, w_ref, sems,
):
    me = lax.axis_index("head")
    copies = []
    for shift in range(4):
        at = pl.multiple_of(((me + shift) & 3) * 512, 512)
        copies.append(
            pltpu.make_async_copy(w_hbm.at[:, pl.ds(at, 512)], w_ref.at[shift], sems.at[shift])
        )
    for copy in copies:
        copy.start()
    total = None
    outs = (mix0_ref, mix1_ref, mix2_ref, mix3_ref)
    for shift, og_ref in enumerate((og0_ref, og1_ref, og2_ref, og3_ref)):
        copies[shift].wait()
        w = w_ref[shift]
        outs[shift][...] = dot(att_ref[...], w, NN).astype(BF)
        term = dot(og_ref[...], w, NT)
        total = term if shift == 0 else total + term
    gatt_ref[...] = total.astype(BF)


def route_kernel(mine_ref, got_ref, own_ref, up_ref, down_ref, across_ref):
    me = lax.axis_index("dp")
    for shift, out in ((0, own_ref), (1, up_ref), (3, down_ref), (2, across_ref)):
        i = (me + shift) & 3
        out[...] = (mine_ref[i].astype(F32) + got_ref[i].astype(F32)).astype(BF)


def bwd_kernel(
    _, q_ref, da_ref, att_ref, exps_ref, fexps_ref, keys_ref, vals_ref, fkeys_ref, fvals_ref,
    rnear_ref, rfar_ref,
    dq_ref, mid_ref, edge_ref, own_ref, cross_ref, minec_ref, gk_ref, gv_ref,
):
    c = lax.axis_index("core")
    by_near, by_far = top_near(), top_far()
    for h in range(HEADS):
        at_h = slice(h * DH, (h + 1) * DH)
        q, da = q_ref[:, at_h], da_ref[:, at_h]
        att = att_ref[:, at_h].astype(F32)
        delta = jnp.sum(da.astype(F32) * att, axis=1, keepdims=True)
        p = fexps_ref[h].astype(F32) * rfar_ref[h]
        pgrad = dot(da, fvals_ref[h], NT)
        sgrad = (p * ((pgrad - delta) * SCALE)).astype(BF)
        dq = dot(sgrad, fkeys_ref[h], NN)
        fgk, fgv = dot(sgrad, q, TN), dot(p.astype(BF), da, TN)
        gk, gv = gk_ref.at[h], gv_ref.at[h]
        gk[512:640] = jnp.zeros((128, DH), F32)
        gv[512:640] = jnp.zeros((128, DH), F32)
        for n in range(2):
            rows = slice(n * NR, (n + 1) * NR)
            span = slice(n * NR, n * NR + JOINT)
            p = exps_ref[h, n].astype(F32) * rnear_ref[h, rows]
            pgrad = dot(da[rows], vals_ref[h, span], NT)
            sgrad = (p * ((pgrad - delta[rows]) * SCALE)).astype(BF)
            p = p.astype(BF)
            dq_ref[rows, at_h] = (dq[rows] + dot(sgrad, keys_ref[h, span], NN)).astype(BF)
            if n == 0:
                gk[0:512] = dot(sgrad, q[rows], TN)
                gv[0:512] = dot(p, da[rows], TN)
            else:
                gk[128:640] += dot(sgrad, q[rows], TN)
                gv[128:640] += dot(p, da[rows], TN)
        for part, g, f in ((0, gk, fgk), (1, gv, fgv)):
            high = f[192:256]
            hi = high.astype(BF)
            lo = (high - hi.astype(F32)).astype(BF)
            near = g[384:512] + dot(by_near, hi, TN) + dot(by_near, lo, TN)
            far = f[0:192] + dot(by_far, hi, TN) + dot(by_far, lo, TN)
            before, after = g[0:128].astype(BF), g[512:640].astype(BF)
            edge_ref[part, :, at_h] = jnp.where(c == 0, before, after)
            cross_ref[part, 160:288, at_h] = jnp.where(c == 0, after, before)
            mid_ref[part, :, at_h] = g[128:384]
            own_ref[part, :, at_h] = near[0:64]
            cross_ref[part, 0:64, at_h] = near[64:128].astype(BF)
            cross_ref[part, 64:96, at_h] = far[32:64].astype(BF)
            minec_ref[part, 0:32, at_h] = far[0:32]
            for d in (2, 3):
                at, to = 64 + (d - 2) * 32, 32 + (d - 2) * 16
                minec_ref[part, to : to + 16, at_h] = far[at : at + 16]
                cross_ref[part, 64 + to : 64 + to + 16, at_h] = far[at + 16 : at + 32].astype(BF)
            for d in (4, 6):
                at, to = 128 + (d - 4) * 16, 64 + (d - 4) * 8
                minec_ref[part, to : to + 8, at_h] = far[at : at + 8]
                minec_ref[part, to + 8 : to + 16, at_h] = far[at + 16 : at + 24]
                both = jnp.concatenate([far[at + 8 : at + 16], far[at + 24 : at + 32]], axis=0)
                cross_ref[part, 64 + to : 64 + to + 16, at_h] = both.astype(BF)


def merge_kernel(_, wsum_ref, minec_ref, got_ref, near_ref, out_ref):
    z = lax.axis_index("z")
    out_ref[:, 0:128] = wsum_ref[...]
    none = jnp.zeros((128, 128), BF)
    out_ref[z, 128:256] = none
    out_ref[z ^ 1, 128:256] = none
    for part in range(2):
        total = (minec_ref[part] + got_ref[part, 64:160].astype(F32)).astype(BF)
        near_ref[part] = total[0:32]
        low = total[64:96]
        for d in range(2, 8):
            if d < 4:
                piece = total[32 + (d - 2) * 16 : 48 + (d - 2) * 16]
            else:
                piece = low[(d - 4) * 8 : (d - 4) * 8 + 8]
                piece = jnp.concatenate([piece, jnp.zeros((8, WIDTH), BF)], axis=0)
            for col in range(4):
                at = 128 + part * 64 + col * 16
                out_ref[z ^ d, at : at + 16] = piece[:, col * 128 : (col + 1) * 128]


def sum_kernel(a_ref, b_ref, c_ref, d_ref, out_ref):
    total = a_ref[...].astype(F32) + b_ref[...].astype(F32)
    total = total + c_ref[...].astype(F32) + d_ref[...].astype(F32)
    out_ref[...] = total.astype(BF)


def mixed_kernel(a_ref, b_ref, c_ref, d_ref, out_ref, token_ref):
    sum_kernel(a_ref, b_ref, c_ref, d_ref, out_ref)
    token_ref[...] = jnp.zeros_like(token_ref)


def sum8_kernel(a_ref, out_ref):
    total = a_ref[0, 0:128].astype(F32)
    for j in range(1, 8):
        total = total + a_ref[j, 0:128].astype(F32)
    out_ref[...] = total.astype(BF)


def collect_kernel(_, __, a_ref, b_ref, c_ref, d_ref, out_ref):
    me = lax.axis_index("dp")
    for shift, ref in ((0, a_ref), (1, b_ref), (2, c_ref), (3, d_ref)):
        out_ref[(me + shift) & 3] = ref[...].astype(F32)


def final_kernel(
    mid_ref, own_ref, got_ref, near_ref, far_ref, edge_ref, _,
    gk_ref, gv_ref, token_ref,
):
    z, c = lax.axis_index("z"), lax.axis_index("core")
    m = pool_matrix(128, ROWS, flip=True)
    for part, out in ((0, gk_ref), (1, gv_ref)):
        l0 = own_ref[part] + got_ref[part, 0:64].astype(F32)
        l1 = near_ref[part].astype(F32)
        base = 128 + part * 64
        far = [far_ref[z ^ d, base : base + 64].astype(F32) for d in range(2, 8)]
        l2, l3 = far[0] + far[1], far[2] + far[3] + far[4] + far[5]
        l2 = jnp.concatenate([l2[i * 16 : (i + 1) * 16] for i in range(4)], axis=1)
        l3 = jnp.concatenate([l3[i * 16 : (i + 1) * 16] for i in range(4)], axis=1)
        stack = jnp.concatenate([l0, l1, l2, l3], axis=0)
        hi = stack.astype(BF)
        lo = (stack - hi.astype(F32)).astype(BF)
        spread = dot(m, hi, NN) + dot(m, lo, NN)
        total = mid_ref[part] + spread
        beside, across = got_ref[part, 160:288].astype(F32), edge_ref[part].astype(F32)
        out[0:128] = (total[0:128] + jnp.where(c == 0, across, beside)).astype(BF)
        out[128:256] = (total[128:256] + jnp.where(c == 0, beside, across)).astype(BF)
    token_ref[...] = jnp.zeros_like(token_ref)


def sds(shape, dtype):
    return jax.ShapeDtypeStruct(shape, dtype)


TOKEN = sds((8, 128), F32)


HBM = pl.BlockSpec(memory_space=pltpu.HBM)
VMEM = pl.BlockSpec(memory_space=pltpu.VMEM)
AFTER = pl.BlockSpec(memory_space=pl.ANY)


def call(kernel, operands, outs, scratch=(), us=1, limit=LIMIT):
    return pl.pallas_call(
        kernel,
        out_shape=outs,
        in_specs=[spec for spec, _ in operands],
        out_specs=[VMEM] * len(outs),
        scratch_shapes=list(scratch),
        compiler_params=pltpu.CompilerParams(vmem_limit_bytes=limit),
        cost_estimate=pl.CostEstimate(flops=us * 10**9, bytes_accessed=1, transcendentals=0),
    )(*[array for _, array in operands])


def here(*arrays):
    return [(VMEM, array) for array in arrays]


def permute(x, axis, move):
    size = lax.axis_size(axis)
    return lax.ppermute(x, axis, [(i, move(i) % size) for i in range(size)])


def body(queries, keys, values, out_weight, out_grad):
    q, k, v = (x.reshape(ROWS, WIDTH) for x in (queries, keys, values))
    n_seq = 2 * lax.axis_size("z")
    pairs = [(i, i + 1) for i in range(1, n_seq - 1, 2)]
    pairs += [(j, i) for i, j in pairs]
    outer = functools.partial(lax.ppermute, axis_name=("z", "core"), perm=pairs)
    swap = functools.partial(permute, axis="core", move=lambda i: i ^ 1)
    hop = functools.partial(permute, axis="z", move=lambda i: i ^ 1)
    dma = pltpu.SemaphoreType.DMA

    og = out_grad.reshape(ROWS, WIDTH)

    chip, near, far, edge = call(
        prep_kernel, [(HBM, k), (HBM, v)],
        [sds((2, 192, WIDTH), BF), sds((2, 32, WIDTH), BF), sds((8, 2, 16, WIDTH), BF),
         sds((2, NR, WIDTH), BF)],
        [pltpu.VMEM((2, ROWS, WIDTH), BF), dma((2,))], limit=62 * 1024 * 1024,
    )
    sib = swap(chip)
    near_got = hop(near)
    near_other = swap(near_got)
    edge_got = outer(edge)
    far_got = lax.all_to_all(far, "z", 0, 0)
    far_other = swap(far_got)
    ogs = [og] + [permute(og, "head", lambda i, m=m: i - m) for m in (1, 2, 3)]

    (token,) = call(token_kernel, [(AFTER, x) for x in ogs[1:]], [sds((8, 128), F32)], us=10)

    column = sds((HEADS, ROWS, 1), F32)
    keys_near, vals_near, exps, part, top, total = call(
        near_kernel, [(AFTER, token)] + here(q, k, v, edge_got, chip, sib),
        [sds((HEADS, NEAR, DH), BF), sds((HEADS, NEAR, DH), BF), sds((HEADS, 2, NR, JOINT), BF),
         sds((ROWS, WIDTH), F32), column, column],
        us=20,
    )
    att, attt, far_exps, keys_far, vals_far, rnear, rfar = call(
        far_kernel, here(q, near_got, near_other, far_got, far_other, keys_near, vals_near, part, top, total),
        [sds((ROWS, WIDTH), BF), sds((WIDTH, ROWS), BF), sds((HEADS, ROWS, FAR), BF),
         sds((HEADS, FAR, DH), BF), sds((HEADS, FAR, DH), BF), column, column],
    )
    mine, theirs = call(wgrad_kernel, here(attt, *ogs), [sds((4, 8, 128, 128), BF)] * 2)
    got = swap(theirs)
    *mixes, gatt = call(
        proj_kernel, [(AFTER, mine), (VMEM, att), (HBM, out_weight)] + here(*ogs),
        [sds((ROWS, WIDTH), BF)] * 5, [pltpu.VMEM((4, WIDTH, 512), BF), dma((4,))],
    )
    mix_parts = [mixes[0]]
    mix_parts += [permute(mixes[m], "head", lambda i, m=m: i + m) for m in (2, 1, 3)]

    kept, to_up, to_down, to_across = call(
        route_kernel, here(mine, got), [sds((8, 128, 128), BF)] * 4
    )
    from_across = permute(to_across, "dp", lambda i: i + 2)
    from_down = permute(to_up, "dp", lambda i: i + 1)
    from_up = permute(to_down, "dp", lambda i: i - 1)

    dq, mid, edge_grad, own_grad, cross, minec = call(
        bwd_kernel,
        [(AFTER, kept)]
        + here(q, gatt, att, exps, far_exps, keys_near, vals_near, keys_far, vals_far)
        + here(rnear, rfar),
        [sds((ROWS, WIDTH), BF), sds((2, ROWS, WIDTH), F32), sds((2, NR, WIDTH), BF),
         sds((2, 64, WIDTH), F32), sds((2, 288, WIDTH), BF),
         sds((2, 96, WIDTH), F32)],
        [pltpu.VMEM((HEADS, NEAR, DH), F32)] * 2, us=20,
    )
    cross_got = swap(cross)
    edge_back = outer(edge_grad)
    (wsum,) = call(
        sum_kernel, here(kept, from_across, from_down, from_up), [sds((8, 128, 128), BF)], us=8
    )
    near_grad, both = call(
        merge_kernel, [(AFTER, edge_back)] + here(wsum, minec, cross_got),
        [sds((2, 32, WIDTH), BF), sds((8, 256, 128), BF)],
    )
    near_back = hop(near_grad)
    both_got = lax.all_to_all(both, "z", 0, 0)
    (wpart,) = call(
        sum8_kernel, here(both_got), [sds((128, 128), BF)], us=20
    )
    mixed, token_mixed = call(
        mixed_kernel, here(*mix_parts), [sds((ROWS, WIDTH), BF), TOKEN],
    )
    wparts = [wpart] + [permute(wpart, "dp", lambda i, m=m: i - m) for m in (1, 2, 3)]

    grad_keys, grad_values, token_keys = call(
        final_kernel,
        here(mid, own_grad, cross_got, near_back, both_got, edge_back)
        + [(AFTER, wpart)],
        [sds((ROWS, WIDTH), BF)] * 2 + [TOKEN],
    )
    (wall,) = call(
        collect_kernel, [(AFTER, token_mixed), (AFTER, token_keys)] + here(*wparts),
        [sds((4, 128, 128), F32)],
    )
    grad_out_weight = wall.reshape(WIDTH, 128)
    shape = (1, ROWS, WIDTH)
    return (
        mixed.reshape(shape), dq.reshape(shape), grad_keys.reshape(shape),
        grad_values.reshape(shape), grad_out_weight,
    )


def solution(mesh):
    dp, seq, head = (mesh.shape[name] for name in ("dp", "seq", "head"))
    cut = Mesh(mesh.devices.reshape(dp, seq // 2, 2, head), ("dp", "z", "core", "head"))
    rows = P("dp", ("z", "core"), "head")
    return jax.shard_map(
        body,
        mesh=cut,
        in_specs=(rows, rows, rows, P("head", None), rows),
        out_specs=(rows, rows, rows, rows, P("head", ("z", "core"))),
        check_vma=False,
    )
```

```python
import functools
import math

import jax
import jax.numpy as jnp
from jax import lax
from jax.experimental import pallas as pl
from jax.experimental.pallas import tpu as pltpu
from jax.sharding import Mesh, PartitionSpec as P

DH = 128
NR = 128
C = 64
HEADS = 4
ROWS = 256
WIDTH = 512
NEAR = 640
JOINT = 512
FAR = 256
BF = jnp.bfloat16
F32 = jnp.float32
LIMIT = 36 * 1024 * 1024
SCALE = 1.0 / math.sqrt(DH)
LOG2E = math.log2(math.e)


def pool_matrix(rows, positions, flip=False):
    shape = (positions, rows) if flip else (rows, positions)
    r = lax.broadcasted_iota(jnp.int32, shape, 1 if flip else 0)
    p = lax.broadcasted_iota(jnp.int32, shape, 0 if flip else 1)
    l0 = (r < 64) & ((p >> 2) == r)
    l1 = (r >= 64) & (r < 96) & ((p >> 3) == r - 64)
    l2 = (r >= 96) & (r < 112) & ((p >> 4) == r - 96)
    l3 = (r >= 112) & (r < 120) & ((p >> 5) == r - 112)
    out = jnp.where(l0, 0.25, 0.0) + jnp.where(l1, 0.125, 0.0)
    out = out + jnp.where(l2, 0.0625, 0.0) + jnp.where(l3, 0.03125, 0.0)
    return out.astype(BF)


def top_near():
    r = lax.broadcasted_iota(jnp.int32, (64, 128), 0)
    j = lax.broadcasted_iota(jnp.int32, (64, 128), 1)
    return jnp.where((j >> 4) == r, 0.0625, 0.0).astype(BF)


def top_far():
    r = lax.broadcasted_iota(jnp.int32, (64, 192), 0)
    j = lax.broadcasted_iota(jnp.int32, (64, 192), 1)
    l1 = (j < 64) & (8 + (j >> 3) == r)
    l2 = (j >= 64) & (j < 128) & (16 + ((j - 64) >> 2) == r)
    l3 = (j >= 128) & (32 + ((j - 128) >> 1) == r)
    out = jnp.where(l1, 0.125, 0.0) + jnp.where(l2, 0.25, 0.0) + jnp.where(l3, 0.5, 0.0)
    return out.astype(BF)


def dot(a, b, dims):
    return lax.dot_general(a, b, (dims, ((), ())), preferred_element_type=F32)


NN = ((1,), (0,))
NT = ((1,), (1,))
TN = ((0,), (0,))


def prep_kernel(k_hbm, v_hbm, chip_ref, near_ref, far_ref, edge_ref, held, sems):
    z, c = lax.axis_index("z"), lax.axis_index("core")
    copies = [
        pltpu.make_async_copy(src, held.at[at], sems.at[at])
        for at, src in ((0, k_hbm), (1, v_hbm))
    ]
    for copy in copies:
        copy.start()
    m = pool_matrix(128, ROWS)
    for part in range(2):
        copies[part].wait()
        x = held[part]
        pooled = dot(m, x, NN).astype(BF)
        chip_ref[part, 0:64] = pooled[0:64]
        near_ref[part] = pooled[64:96]
        for d in range(8):
            far_ref[z ^ d, part] = pooled[112:128] if d >= 4 else pooled[96:112]
        chip_ref[part, 64:192] = jnp.where(c == 0, x[NR:], x[:NR])
        edge_ref[part] = jnp.where(c == 0, x[:NR], x[NR:])


def token_kernel(_, __, ___, out_ref):
    out_ref[...] = jnp.zeros_like(out_ref)


def near_kernel(
    _, q_ref, k_ref, v_ref, edge_ref, chip_ref, sib_ref,
    keys_ref, vals_ref, exps_ref, part_ref, max_ref, sum_ref,
):
    z, c = lax.axis_index("z"), lax.axis_index("core")
    s = z * 2 + c
    col = lax.broadcasted_iota(jnp.int32, (1, JOINT), 1)
    for h in range(HEADS):
        at_h = slice(h * DH, (h + 1) * DH)
        for part, own_ref, out in ((0, k_ref, keys_ref), (1, v_ref, vals_ref)):
            beside, across = sib_ref[part, 64:192, at_h], edge_ref[part, :, at_h]
            out[h, 0:128] = jnp.where(c == 0, across, beside)
            out[h, 128:384] = own_ref[:, at_h]
            out[h, 384:448] = chip_ref[part, 0:64, at_h]
            out[h, 448:512] = sib_ref[part, 0:64, at_h]
            out[h, 512:640] = jnp.where(c == 0, beside, across)
        for n in range(2):
            rows = slice(n * NR, (n + 1) * NR)
            span = slice(n * NR, n * NR + JOINT)
            scores = dot(q_ref[rows, at_h], keys_ref[h, span], NT)
            if n == 0:
                hidden = (col < NR) & (s == 0)
            else:
                hidden = (col >= JOINT - NR) & (s == 15)
            scores = jnp.where(hidden, -jnp.inf, scores)
            highest = jnp.max(scores, axis=1, keepdims=True)
            e = jnp.exp2((scores - highest) * (SCALE * LOG2E))
            max_ref[h, rows] = highest
            sum_ref[h, rows] = jnp.sum(e, axis=1, keepdims=True)
            e = e.astype(BF)
            exps_ref[h, n] = e
            part_ref[rows, at_h] = dot(e, vals_ref[h, span], NN)


def far_kernel(
    q_ref, near_ref, nearo_ref, far_ref, faro_ref, keys_ref, vals_ref, part_ref, max_ref, sum_ref,
    att_ref, attt_ref, exps_ref, fkeys_ref, fvals_ref, rnear_ref, rfar_ref,
):
    z = lax.axis_index("z")
    by_near, by_far = top_near(), top_far()
    for h in range(HEADS):
        at_h = slice(h * DH, (h + 1) * DH)
        for part, near, out in ((0, keys_ref, fkeys_ref), (1, vals_ref, fvals_ref)):
            out[h, 0:32] = near_ref[part, :, at_h]
            out[h, 32:64] = nearo_ref[part, :, at_h]
            for d in (2, 3):
                at = 64 + (d - 2) * 32
                out[h, at : at + 16] = far_ref[z ^ d, part, :, at_h]
                out[h, at + 16 : at + 32] = faro_ref[z ^ d, part, :, at_h]
            for d in range(4, 8):
                at = 128 + (d - 4) * 16
                low, high = far_ref[z ^ d, part, :, at_h], faro_ref[z ^ d, part, :, at_h]
                out[h, at : at + 16] = jnp.concatenate([low[0:8], high[0:8]], axis=0)
            top = dot(by_near, near[h, 384:512], NN) + dot(by_far, out[h, 0:192], NN)
            out[h, 192:256] = top.astype(BF)
        scores = dot(q_ref[:, at_h], fkeys_ref[h], NT)
        first = max_ref[h]
        highest = jnp.maximum(first, jnp.max(scores, axis=1, keepdims=True))
        e = jnp.exp2((scores - highest) * (SCALE * LOG2E))
        kept = jnp.exp2((first - highest) * (SCALE * LOG2E))
        inverse = 1.0 / (kept * sum_ref[h] + jnp.sum(e, axis=1, keepdims=True))
        e = e.astype(BF)
        exps_ref[h] = e
        rnear_ref[h] = kept * inverse
        rfar_ref[h] = inverse
        att = part_ref[:, at_h] * (kept * inverse) + dot(e, fvals_ref[h], NN) * inverse
        att_ref[:, at_h] = att.astype(BF)
        attt_ref[at_h, :] = att.T.astype(BF)


def wgrad_kernel(attt_ref, og0_ref, og1_ref, og2_ref, og3_ref, mine_ref, theirs_ref):
    c, me = lax.axis_index("core"), lax.axis_index("head")
    for shift, og_ref in enumerate((og0_ref, og1_ref, og2_ref, og3_ref)):
        j = (me + shift) & 3
        r = dot(attt_ref[...], og_ref[...], NN).astype(BF)
        for i in range(4):
            for t in range(2):
                lo = r[i * 128 : (i + 1) * 128, t * 256 : t * 256 + 128]
                hi = r[i * 128 : (i + 1) * 128, t * 256 + 128 : t * 256 + 256]
                mine_ref[i, 2 * j + t] = jnp.where(c == 0, lo, hi)
                theirs_ref[i, 2 * j + t] = jnp.where(c == 0, hi, lo)


def proj_kernel(
    _, att_ref, w_hbm, og0_ref, og1_ref, og2_ref, og3_ref,
    mix0_ref, mix1_ref, mix2_ref, mix3_ref, gatt_ref, w_ref, sems,
):
    me = lax.axis_index("head")
    copies = []
    for shift in range(4):
        at = pl.multiple_of(((me + shift) & 3) * 512, 512)
        copies.append(
            pltpu.make_async_copy(w_hbm.at[:, pl.ds(at, 512)], w_ref.at[shift], sems.at[shift])
        )
    for copy in copies:
        copy.start()
    total = None
    outs = (mix0_ref, mix1_ref, mix2_ref, mix3_ref)
    for shift, og_ref in enumerate((og0_ref, og1_ref, og2_ref, og3_ref)):
        copies[shift].wait()
        w = w_ref[shift]
        outs[shift][...] = dot(att_ref[...], w, NN).astype(BF)
        term = dot(og_ref[...], w, NT)
        total = term if shift == 0 else total + term
    gatt_ref[...] = total.astype(BF)


def route_kernel(mine_ref, got_ref, own_ref, up_ref, down_ref, across_ref):
    me = lax.axis_index("dp")
    for shift, out in ((0, own_ref), (1, up_ref), (3, down_ref), (2, across_ref)):
        i = (me + shift) & 3
        out[...] = (mine_ref[i].astype(F32) + got_ref[i].astype(F32)).astype(BF)


def bwd_kernel(
    _, q_ref, da_ref, att_ref, exps_ref, fexps_ref, keys_ref, vals_ref, fkeys_ref, fvals_ref,
    rnear_ref, rfar_ref,
    dq_ref, mid_ref, edge_ref, own_ref, cross_ref, minec_ref, gk_ref, gv_ref,
):
    c = lax.axis_index("core")
    by_near, by_far = top_near(), top_far()
    for h in range(HEADS):
        at_h = slice(h * DH, (h + 1) * DH)
        q, da = q_ref[:, at_h], da_ref[:, at_h]
        att = att_ref[:, at_h].astype(F32)
        delta = jnp.sum(da.astype(F32) * att, axis=1, keepdims=True)
        p = fexps_ref[h].astype(F32) * rfar_ref[h]
        pgrad = dot(da, fvals_ref[h], NT)
        sgrad = (p * ((pgrad - delta) * SCALE)).astype(BF)
        dq = dot(sgrad, fkeys_ref[h], NN)
        fgk, fgv = dot(sgrad, q, TN), dot(p.astype(BF), da, TN)
        gk, gv = gk_ref.at[h], gv_ref.at[h]
        gk[512:640] = jnp.zeros((128, DH), F32)
        gv[512:640] = jnp.zeros((128, DH), F32)
        for n in range(2):
            rows = slice(n * NR, (n + 1) * NR)
            span = slice(n * NR, n * NR + JOINT)
            p = exps_ref[h, n].astype(F32) * rnear_ref[h, rows]
            pgrad = dot(da[rows], vals_ref[h, span], NT)
            sgrad = (p * ((pgrad - delta[rows]) * SCALE)).astype(BF)
            p = p.astype(BF)
            dq_ref[rows, at_h] = (dq[rows] + dot(sgrad, keys_ref[h, span], NN)).astype(BF)
            if n == 0:
                gk[0:512] = dot(sgrad, q[rows], TN)
                gv[0:512] = dot(p, da[rows], TN)
            else:
                gk[128:640] += dot(sgrad, q[rows], TN)
                gv[128:640] += dot(p, da[rows], TN)
        for part, g, f in ((0, gk, fgk), (1, gv, fgv)):
            high = f[192:256]
            hi = high.astype(BF)
            lo = (high - hi.astype(F32)).astype(BF)
            near = g[384:512] + dot(by_near, hi, TN) + dot(by_near, lo, TN)
            far = f[0:192] + dot(by_far, hi, TN) + dot(by_far, lo, TN)
            before, after = g[0:128].astype(BF), g[512:640].astype(BF)
            edge_ref[part, :, at_h] = jnp.where(c == 0, before, after)
            cross_ref[part, 160:288, at_h] = jnp.where(c == 0, after, before)
            mid_ref[part, :, at_h] = g[128:384]
            own_ref[part, :, at_h] = near[0:64]
            cross_ref[part, 0:64, at_h] = near[64:128].astype(BF)
            cross_ref[part, 64:96, at_h] = far[32:64].astype(BF)
            minec_ref[part, 0:32, at_h] = far[0:32]
            for d in (2, 3):
                at, to = 64 + (d - 2) * 32, 32 + (d - 2) * 16
                minec_ref[part, to : to + 16, at_h] = far[at : at + 16]
                cross_ref[part, 64 + to : 64 + to + 16, at_h] = far[at + 16 : at + 32].astype(BF)
            for d in (4, 6):
                at, to = 128 + (d - 4) * 16, 64 + (d - 4) * 8
                minec_ref[part, to : to + 8, at_h] = far[at : at + 8]
                minec_ref[part, to + 8 : to + 16, at_h] = far[at + 16 : at + 24]
                both = jnp.concatenate([far[at + 8 : at + 16], far[at + 24 : at + 32]], axis=0)
                cross_ref[part, 64 + to : 64 + to + 16, at_h] = both.astype(BF)


def gather_kernel(minec_ref, got_ref, near_ref, out_ref):
    z = lax.axis_index("z")
    none = jnp.zeros((128, 128), BF)
    out_ref[z] = none
    out_ref[z ^ 1] = none
    for part in range(2):
        total = (minec_ref[part] + got_ref[part, 64:160].astype(F32)).astype(BF)
        near_ref[part] = total[0:32]
        low = total[64:96]
        for d in range(2, 8):
            if d < 4:
                piece = total[32 + (d - 2) * 16 : 48 + (d - 2) * 16]
            else:
                piece = low[(d - 4) * 8 : (d - 4) * 8 + 8]
                piece = jnp.concatenate([piece, jnp.zeros((8, WIDTH), BF)], axis=0)
            for col in range(4):
                at = part * 64 + col * 16
                out_ref[z ^ d, at : at + 16] = piece[:, col * 128 : (col + 1) * 128]


def merge_kernel(_, wsum_ref, far_ref, out_ref):
    out_ref[:, 0:128] = wsum_ref[...]
    out_ref[:, 128:256] = far_ref[...]


def sum_kernel(a_ref, b_ref, c_ref, d_ref, out_ref):
    total = a_ref[...].astype(F32) + b_ref[...].astype(F32)
    total = total + c_ref[...].astype(F32) + d_ref[...].astype(F32)
    out_ref[...] = total.astype(BF)


def mixed_kernel(a_ref, b_ref, c_ref, d_ref, out_ref, token_ref):
    sum_kernel(a_ref, b_ref, c_ref, d_ref, out_ref)
    token_ref[...] = jnp.zeros_like(token_ref)


def sum8_kernel(a_ref, out_ref):
    total = a_ref[0, 0:128].astype(F32)
    for j in range(1, 8):
        total = total + a_ref[j, 0:128].astype(F32)
    out_ref[...] = total.astype(BF)


def collect_kernel(_, __, a_ref, b_ref, c_ref, d_ref, out_ref):
    me = lax.axis_index("dp")
    for shift, ref in ((0, a_ref), (1, b_ref), (2, c_ref), (3, d_ref)):
        out_ref[(me + shift) & 3] = ref[...].astype(F32)


def final_kernel(
    mid_ref, own_ref, got_ref, near_ref, far_ref, edge_ref, _,
    gk_ref, gv_ref, token_ref,
):
    z, c = lax.axis_index("z"), lax.axis_index("core")
    m = pool_matrix(128, ROWS, flip=True)
    for part, out in ((0, gk_ref), (1, gv_ref)):
        l0 = own_ref[part] + got_ref[part, 0:64].astype(F32)
        l1 = near_ref[part].astype(F32)
        base = 128 + part * 64
        far = [far_ref[z ^ d, base : base + 64].astype(F32) for d in range(2, 8)]
        l2, l3 = far[0] + far[1], far[2] + far[3] + far[4] + far[5]
        l2 = jnp.concatenate([l2[i * 16 : (i + 1) * 16] for i in range(4)], axis=1)
        l3 = jnp.concatenate([l3[i * 16 : (i + 1) * 16] for i in range(4)], axis=1)
        stack = jnp.concatenate([l0, l1, l2, l3], axis=0)
        hi = stack.astype(BF)
        lo = (stack - hi.astype(F32)).astype(BF)
        spread = dot(m, hi, NN) + dot(m, lo, NN)
        total = mid_ref[part] + spread
        beside, across = got_ref[part, 160:288].astype(F32), edge_ref[part].astype(F32)
        out[0:128] = (total[0:128] + jnp.where(c == 0, across, beside)).astype(BF)
        out[128:256] = (total[128:256] + jnp.where(c == 0, beside, across)).astype(BF)
    token_ref[...] = jnp.zeros_like(token_ref)


def sds(shape, dtype):
    return jax.ShapeDtypeStruct(shape, dtype)


TOKEN = sds((8, 128), F32)


HBM = pl.BlockSpec(memory_space=pltpu.HBM)
VMEM = pl.BlockSpec(memory_space=pltpu.VMEM)
AFTER = pl.BlockSpec(memory_space=pl.ANY)


def call(kernel, operands, outs, scratch=(), us=1, limit=LIMIT):
    return pl.pallas_call(
        kernel,
        out_shape=outs,
        in_specs=[spec for spec, _ in operands],
        out_specs=[VMEM] * len(outs),
        scratch_shapes=list(scratch),
        compiler_params=pltpu.CompilerParams(vmem_limit_bytes=limit),
        cost_estimate=pl.CostEstimate(flops=us * 10**9, bytes_accessed=1, transcendentals=0),
    )(*[array for _, array in operands])


def here(*arrays):
    return [(VMEM, array) for array in arrays]


def permute(x, axis, move):
    size = lax.axis_size(axis)
    return lax.ppermute(x, axis, [(i, move(i) % size) for i in range(size)])


def body(queries, keys, values, out_weight, out_grad):
    q, k, v = (x.reshape(ROWS, WIDTH) for x in (queries, keys, values))
    n_seq = 2 * lax.axis_size("z")
    pairs = [(i, i + 1) for i in range(1, n_seq - 1, 2)]
    pairs += [(j, i) for i, j in pairs]
    outer = functools.partial(lax.ppermute, axis_name=("z", "core"), perm=pairs)
    swap = functools.partial(permute, axis="core", move=lambda i: i ^ 1)
    hop = functools.partial(permute, axis="z", move=lambda i: i ^ 1)
    dma = pltpu.SemaphoreType.DMA

    og = out_grad.reshape(ROWS, WIDTH)

    chip, near, far, edge = call(
        prep_kernel, [(HBM, k), (HBM, v)],
        [sds((2, 192, WIDTH), BF), sds((2, 32, WIDTH), BF), sds((8, 2, 16, WIDTH), BF),
         sds((2, NR, WIDTH), BF)],
        [pltpu.VMEM((2, ROWS, WIDTH), BF), dma((2,))], limit=62 * 1024 * 1024,
    )
    sib = swap(chip)
    near_got = hop(near)
    near_other = swap(near_got)
    edge_got = outer(edge)
    far_got = lax.all_to_all(far, "z", 0, 0)
    far_other = swap(far_got)
    ogs = [og] + [permute(og, "head", lambda i, m=m: i - m) for m in (1, 2, 3)]

    (token,) = call(token_kernel, [(AFTER, x) for x in ogs[1:]], [sds((8, 128), F32)], us=10)

    column = sds((HEADS, ROWS, 1), F32)
    keys_near, vals_near, exps, part, top, total = call(
        near_kernel, [(AFTER, token)] + here(q, k, v, edge_got, chip, sib),
        [sds((HEADS, NEAR, DH), BF), sds((HEADS, NEAR, DH), BF), sds((HEADS, 2, NR, JOINT), BF),
         sds((ROWS, WIDTH), F32), column, column],
        us=20,
    )
    att, attt, far_exps, keys_far, vals_far, rnear, rfar = call(
        far_kernel, here(q, near_got, near_other, far_got, far_other, keys_near, vals_near, part, top, total),
        [sds((ROWS, WIDTH), BF), sds((WIDTH, ROWS), BF), sds((HEADS, ROWS, FAR), BF),
         sds((HEADS, FAR, DH), BF), sds((HEADS, FAR, DH), BF), column, column],
    )
    mine, theirs = call(wgrad_kernel, here(attt, *ogs), [sds((4, 8, 128, 128), BF)] * 2)
    got = swap(theirs)
    *mixes, gatt = call(
        proj_kernel, [(AFTER, mine), (VMEM, att), (HBM, out_weight)] + here(*ogs),
        [sds((ROWS, WIDTH), BF)] * 5, [pltpu.VMEM((4, WIDTH, 512), BF), dma((4,))],
    )
    mix_parts = [mixes[0]]
    mix_parts += [permute(mixes[m], "head", lambda i, m=m: i + m) for m in (2, 1, 3)]

    kept, to_up, to_down, to_across = call(
        route_kernel, here(mine, got), [sds((8, 128, 128), BF)] * 4
    )
    from_across = permute(to_across, "dp", lambda i: i + 2)
    from_down = permute(to_up, "dp", lambda i: i + 1)
    from_up = permute(to_down, "dp", lambda i: i - 1)

    dq, mid, edge_grad, own_grad, cross, minec = call(
        bwd_kernel,
        [(AFTER, kept)]
        + here(q, gatt, att, exps, far_exps, keys_near, vals_near, keys_far, vals_far)
        + here(rnear, rfar),
        [sds((ROWS, WIDTH), BF), sds((2, ROWS, WIDTH), F32), sds((2, NR, WIDTH), BF),
         sds((2, 64, WIDTH), F32), sds((2, 288, WIDTH), BF),
         sds((2, 96, WIDTH), F32)],
        [pltpu.VMEM((HEADS, NEAR, DH), F32)] * 2, us=20,
    )
    cross_got = swap(cross)
    edge_back = outer(edge_grad)
    (wsum,) = call(
        sum_kernel, here(kept, from_across, from_down, from_up), [sds((8, 128, 128), BF)], us=8
    )
    near_grad, far_grad = call(
        gather_kernel, here(minec, cross_got),
        [sds((2, 32, WIDTH), BF), sds((8, 128, 128), BF)],
    )
    (both,) = call(
        merge_kernel, [(AFTER, edge_back)] + here(wsum, far_grad), [sds((8, 256, 128), BF)]
    )
    near_back = hop(near_grad)
    both_got = lax.all_to_all(both, "z", 0, 0)
    (wpart,) = call(
        sum8_kernel, here(both_got), [sds((128, 128), BF)], us=20
    )
    mixed, token_mixed = call(
        mixed_kernel, here(*mix_parts), [sds((ROWS, WIDTH), BF), TOKEN],
    )
    wparts = [wpart] + [permute(wpart, "dp", lambda i, m=m: i - m) for m in (1, 2, 3)]

    grad_keys, grad_values, token_keys = call(
        final_kernel,
        here(mid, own_grad, cross_got, near_back, both_got, edge_back)
        + [(AFTER, wpart)],
        [sds((ROWS, WIDTH), BF)] * 2 + [TOKEN],
    )
    (wall,) = call(
        collect_kernel, [(AFTER, token_mixed), (AFTER, token_keys)] + here(*wparts),
        [sds((4, 128, 128), F32)],
    )
    grad_out_weight = wall.reshape(WIDTH, 128)
    shape = (1, ROWS, WIDTH)
    return (
        mixed.reshape(shape), dq.reshape(shape), grad_keys.reshape(shape),
        grad_values.reshape(shape), grad_out_weight,
    )


def solution(mesh):
    dp, seq, head = (mesh.shape[name] for name in ("dp", "seq", "head"))
    cut = Mesh(mesh.devices.reshape(dp, seq // 2, 2, head), ("dp", "z", "core", "head"))
    rows = P("dp", ("z", "core"), "head")
    return jax.shard_map(
        body,
        mesh=cut,
        in_specs=(rows, rows, rows, P("head", None), rows),
        out_specs=(rows, rows, rows, rows, P("head", ("z", "core"))),
        check_vma=False,
    )
```
